32 devices in a mesh: groups: 2 (over y), dp: 8 (over z, x), tp: 2 (over core).
Axes of the slice: x: 2, y: 2, z: 4, core: 2. Of those that a mesh axis runs over, the one named last changes fastest.
Arguments:
- cache: bfloat16 [32, 1536, 576], P(('groups', 'dp', 'tp')), parts along dimension 0, may hold values from -4 to 4
- lengths: int32 [32], P('groups'), parts along dimension 0, may hold values from 2 to 1535, as said below
- swap_flags: int32 [1, 32], P(None, 'groups'), parts along dimension 1, may hold values from 0 to 1, as said below
- queries: bfloat16 [1, 32, 128, 576], P(None, ('groups', 'dp', 'tp')), parts along dimension 1, may hold values from -20 to 20
- latents: bfloat16 [1, 32, 576], P(None, ('groups', 'dp', 'tp')), parts along dimension 1, may hold values from -4 to 4
- residual: bfloat16 [1, 32, 7168], P(None, ('groups', 'dp', 'tp')), parts along dimension 1, may hold values from -3 to 3
- norm_gain: bfloat16 [7168], replicated, may hold values from 0.5 to 1.5
- value_expand_weight: bfloat16 [128, 512, 128], P(('dp', 'tp')), may hold values from -0.5 to 0.5
- out_proj: bfloat16 [16384, 7168], P(('dp', 'tp')), may hold values from -0.046875 to 0.046875
- gate_weight: bfloat16 [7168, 18432], P(None, ('dp', 'tp')), may hold values from -0.0625 to 0.0625
- up_weight: bfloat16 [7168, 18432], P(None, ('dp', 'tp')), may hold values from -0.0625 to 0.0625
- down_weight: bfloat16 [18432, 7168], P(('dp', 'tp')), may hold values from -0.046875 to 0.046875
Outputs:
- layer_out: bfloat16 [1, 32, 7168], P(None, ('groups', 'dp', 'tp')), parts along dimension 1
- held: bfloat16 [32, 1536, 576], P(('groups', 'dp', 'tp')), parts along dimension 0
The draws below stay inside these ranges and needn't reach their ends.
There are 2 independent parts, one for each index of `groups`. The reference program is written for one: setup_inputs(seed, part) draws one part's arguments, and reference() takes and returns one part's arrays. A program takes and returns all parts, laid end to end along the dimension named above; an argument that names none is the same for every part. Nothing has to cross between parts.
Inputs may be any that keep to these rules, and one draw needn't show every extreme that they name: `lengths`: each row has at least two cached positions, and some row has exactly 1535. `swap_flags`: for each step the flags agree on a slot and its partner slot of that step.
All inputs are finite; a program needn't handle non-finite values.
Results may differ from the reference program's by a relative error of at most 0.0075.
Values may be sent and summed in bfloat16 or wider, within the bound.
No kernel may reach another device: no remote copies, remote signals or barrier semaphores. Data moves between devices by JAX's collectives and lax.ppermute only.
A program may use at most 192 MiB of HBM per device.

```python
import jax
import jax.numpy as jnp
from jax import lax

D = 7168
FF = 18432
HEAD_COUNT = 128
LATENT_WIDTH = 512
VALUE_WIDTH = 128
CTX = 1536
STEPS = 1
RDEV = 1
LAT = 576
RANKS = 16
ROWS = 16


def leading_keys(key):
    base = jax.random.normal(jax.random.fold_in(key, 901), (ROWS, LAT), jnp.float32)
    noise = jax.random.normal(jax.random.fold_in(key, 902), (ROWS, LAT), jnp.float32)
    first = jnp.clip(base, -4.0, 4.0)
    second = jnp.clip(base + 0.3 * noise, -4.0, 4.0)
    return (first, second)


def draw_cache(key, part):
    first, second = leading_keys(key)
    key = jax.random.fold_in(key, 11)
    drawn = jnp.clip(jax.random.normal(jax.random.fold_in(key, 2), (ROWS, CTX, LAT), jnp.float32), -4.0, 4.0)
    drawn = drawn.at[:, 0, :].set(first).at[:, 1, :].set(second)
    return drawn.astype(jnp.bfloat16)


def draw_queries(key, part):
    key = jax.random.fold_in(key, 12)
    drawn = jnp.clip(jax.random.normal(key, (STEPS, ROWS, HEAD_COUNT, LAT), jnp.float32), -4.0, 4.0)
    return drawn.astype(jnp.bfloat16)


def draw_lengths(key, part):
    key = jax.random.fold_in(key, 13)
    most = CTX - STEPS
    drawn = jax.random.randint(jax.random.fold_in(key, 1), (ROWS,), 2, most + 1, jnp.int32)
    where_most = jax.random.randint(jax.random.fold_in(key, 2), (), 0, ROWS, jnp.int32)
    return drawn.at[where_most].set(most)


def draw_swap_flags(key, part):
    key = jax.random.fold_in(key, 14)
    top_bit = RANKS.bit_length() - 1
    slots = jnp.arange(ROWS, dtype=jnp.int32)
    ranks = slots // RDEV
    result = []
    for step in range(STEPS):
        bit = top_bit - 1 - step
        lower = jnp.bitwise_and(ranks, ~(1 << bit)) * RDEV + slots % RDEV
        coins = jax.random.randint(jax.random.fold_in(key, step), (ROWS,), 0, 4, jnp.int32)
        result.append((coins[lower] == 0).astype(jnp.int32))
    return jnp.stack(result)


def level_of(stream_key, dims, pieces, low, high):
    loudness, own = 1.0, jax.random.fold_in(stream_key, 6)
    for dim, shards_of in pieces:
        steps = jnp.exp(jax.random.uniform(jax.random.fold_in(own, dim), (shards_of,), jnp.float32, low / len(pieces), high / len(pieces)))
        loudness = loudness * jnp.repeat(steps, dims[dim] // shards_of).reshape([-1 if axis == dim else 1 for axis in range(len(dims))])
    return loudness


def bell_draw(rng, dims, spread, limit, cuts=(), kind=jnp.bfloat16):
    entries = spread * jax.random.normal(rng, dims, jnp.float32)
    if cuts:
        entries = entries * level_of(rng, dims, cuts, -0.22, 0.18)
    return jnp.clip(entries, -limit, limit).astype(kind)


def setup_inputs(seed: int = 0, part: int = 0) -> dict:
    keys = jax.random.split(jax.random.key(seed), 13)
    own_keys = jax.random.split(jax.random.fold_in(keys[12], part), 13)
    cache = draw_cache(jax.random.fold_in(jax.random.fold_in(keys[12], part), 71), part)
    lengths = draw_lengths(jax.random.fold_in(jax.random.fold_in(keys[12], part), 71), part)
    swap_flags = draw_swap_flags(jax.random.fold_in(jax.random.fold_in(keys[12], part), 71), part)
    queries = draw_queries(jax.random.fold_in(jax.random.fold_in(keys[12], part), 71), part)
    latents = bell_draw(own_keys[4], (STEPS, ROWS, LAT), 1.0, 4.0, ((1, 16),))
    residual = bell_draw(own_keys[5], (STEPS, ROWS, D), 0.5, 3.0, ((1, 16),))
    norm_gain = jnp.clip(1.0 + 0.1 * jax.random.normal(keys[6], (D,), jnp.float32), 0.5, 1.5).astype(jnp.bfloat16)
    value_expand_weight = bell_draw(keys[7], (HEAD_COUNT, LATENT_WIDTH, VALUE_WIDTH), 0.09, 0.5, ((0, 16),))
    out_proj = bell_draw(keys[8], (HEAD_COUNT * VALUE_WIDTH, D), (HEAD_COUNT * VALUE_WIDTH) ** -0.5, 0.046875, ((0, 16),))
    gate_weight = bell_draw(keys[9], (D, FF), D ** -0.5, 0.0625, ((1, 16),))
    up_weight = bell_draw(keys[10], (D, FF), D ** -0.5, 0.0625, ((1, 16),))
    down_weight = bell_draw(keys[11], (FF, D), FF ** -0.5, 0.046875, ((0, 16),))
    return dict(cache=cache, lengths=lengths, swap_flags=swap_flags, queries=queries, latents=latents, residual=residual, norm_gain=norm_gain, value_expand_weight=value_expand_weight, out_proj=out_proj, gate_weight=gate_weight, up_weight=up_weight, down_weight=down_weight)


score_scale = 0.07216878364870322

def attend_row(query_row, key_rows, live):
    scores = jnp.dot(query_row, key_rows.T, preferred_element_type=jnp.float32) * score_scale
    positions = jnp.arange(key_rows.shape[0])
    mask = positions[None, :] < live
    scores = jnp.where(mask, scores, -1e+30)
    top = lax.optimization_barrier(jnp.max(scores, axis=-1, keepdims=True))
    weights = jnp.where(mask, jnp.exp(scores - top), 0.0)
    attention_probabilities = (weights / lax.optimization_barrier(jnp.sum(weights, axis=-1, keepdims=True))).astype(jnp.bfloat16)
    return jnp.dot(attention_probabilities, key_rows[:, :LATENT_WIDTH], preferred_element_type=jnp.float32).astype(jnp.bfloat16)

def reference(cache, lengths, swap_flags, queries, latents, residual, norm_gain, value_expand_weight, out_proj, gate_weight, up_weight, down_weight):
    top_bit = RANKS.bit_length() - 1
    slots = jnp.arange(ROWS, dtype=jnp.int32)
    held = cache
    held_len = lengths
    results = []
    for step in range(STEPS):
        bit = top_bit - 1 - step
        partner = ((slots // RDEV ^ 1 << bit) * RDEV + slots % RDEV).astype(jnp.int32)
        moved = jnp.where(swap_flags[step] == 1, partner, slots).astype(jnp.int32)
        held = held[moved]
        held_len = held_len[moved]
        positions = jnp.arange(CTX, dtype=jnp.int32)
        write = positions[None, :] == (held_len + step)[:, None]
        held = jnp.where(write[:, :, None], latents[step][:, None, :], held)
        live = held_len + step + 1
        context_rows = lax.map(lambda item: attend_row(item[0], item[1], item[2]), (queries[step], held, live))
        value_rows = jnp.einsum('wzl,zlb->wzb', context_rows.astype(jnp.float32), value_expand_weight.astype(jnp.float32)).astype(jnp.bfloat16)
        flat = value_rows.reshape(ROWS, HEAD_COUNT * VALUE_WIDTH)
        state = residual[step].astype(jnp.float32) + jnp.dot(flat, out_proj, preferred_element_type=jnp.float32)
        normed = (state * lax.rsqrt(lax.optimization_barrier(jnp.mean(state * state, axis=-1, keepdims=True)) + 1e-06) * norm_gain.astype(jnp.float32)).astype(jnp.bfloat16)
        gate = jnp.dot(normed, gate_weight, preferred_element_type=jnp.float32)
        upper = jnp.dot(normed, up_weight, preferred_element_type=jnp.float32)
        hidden = (jax.nn.silu(gate) * upper).astype(jnp.bfloat16)
        ffn_out = jnp.dot(hidden, down_weight, preferred_element_type=jnp.float32)
        results.append((state + ffn_out).astype(jnp.bfloat16))
    return (jnp.stack(results), held)
```

```python
import jax
import jax.numpy as jnp
from jax import lax
from jax.sharding import PartitionSpec as P

LATENT_WIDTH = 512
AXES = ("dp", "tp")


score_scale = 0.07216878364870322


def swap_bit(block, bit):
    ranks = lax.axis_size(AXES)
    return lax.ppermute(block, AXES, [(rank, rank ^ 1 << bit) for rank in range(ranks)])


def attend(query_rows, key_rows, live):
    scores = (
        jnp.einsum("rhl,rtl->rht", query_rows, key_rows, preferred_element_type=jnp.float32)
        * score_scale
    )
    positions = jnp.arange(key_rows.shape[1])
    mask = positions[None, None, :] < live[:, None, None]
    scores = jnp.where(mask, scores, -1e30)
    top = jnp.max(scores, axis=-1, keepdims=True)
    weights = jnp.where(mask, jnp.exp(scores - top), 0.0)
    attention_probabilities = (weights / jnp.sum(weights, axis=-1, keepdims=True)).astype(
        jnp.bfloat16
    )
    return jnp.einsum(
        "efw,ewa->efa",
        attention_probabilities,
        key_rows[:, :, :LATENT_WIDTH],
        preferred_element_type=jnp.float32,
    ).astype(jnp.bfloat16)


def append_entry(key_rows, entry, where_pos):
    positions = jnp.arange(key_rows.shape[1], dtype=jnp.int32)
    write = positions[None, :] == where_pos[:, None]
    return jnp.where(write[:, :, None], entry[:, None, :], key_rows)


def split_rows(block, bit_value):
    pairs = block.reshape(block.shape[0] // 2, 2, *block.shape[1:])
    keep = lax.dynamic_index_in_dim(pairs, bit_value, 1, keepdims=False)
    send = lax.dynamic_index_in_dim(pairs, 1 - bit_value, 1, keepdims=False)
    return keep, send


def local(
    cache,
    lengths,
    swap_flags,
    queries,
    latents,
    residual,
    norm_gain,
    value_expand_weight,
    out_proj,
    gate_weight,
    up_weight,
    down_weight,
):
    ranks = lax.axis_size(AXES)
    bits = ranks.bit_length() - 1
    rows_dev = cache.shape[0]
    rows_all = rows_dev * ranks
    rank = lax.axis_index(AXES)
    bit_of = [(rank >> bit) & 1 for bit in range(bits)]
    half = rows_all // 2
    top = bits - 1

    flags = swap_flags[0]
    moved_len = jnp.where(flags == 1, jnp.roll(lengths, half), lengths)
    flag_here = lax.dynamic_slice_in_dim(flags, rank * rows_dev, rows_dev, 0) == 1
    len_slot = lax.dynamic_slice_in_dim(moved_len, rank * rows_dev, rows_dev, 0)
    len_own = lax.dynamic_slice_in_dim(lengths, rank * rows_dev, rows_dev, 0)

    query_other = swap_bit(queries[0], top)
    entry_other = swap_bit(latents[0], top)
    query_other, entry_other, cache = lax.optimization_barrier((query_other, entry_other, cache))
    cache_other = swap_bit(cache, top)
    query = jnp.where(flag_here[:, None, None], query_other, queries[0])
    entry = jnp.where(flag_here[:, None], entry_other, latents[0])
    context = attend(query, append_entry(cache, entry, len_own), len_own + 1)

    heads = context.shape[1] // ranks
    per_head = lax.all_to_all(
        context.reshape(rows_dev, ranks, heads, LATENT_WIDTH).swapaxes(0, 1),
        AXES,
        split_axis=0,
        concat_axis=0,
        tiled=True,
    ).reshape(rows_all, heads, LATENT_WIDTH)
    values = jnp.einsum(
        "whl,hlb->whb", per_head, value_expand_weight, preferred_element_type=jnp.float32
    ).astype(jnp.bfloat16)
    values = values.reshape(rows_all, -1)
    values = jnp.where(flags[:, None] == 1, jnp.roll(values, half, axis=0), values)

    partial = jnp.dot(values, out_proj, preferred_element_type=jnp.float32)
    mine = (jnp.arange(rows_all) // rows_dev == rank)[:, None]
    place = jnp.tile(residual[0].astype(jnp.float32), (ranks, 1))
    partial = partial + jnp.where(mine, place, 0.0)

    width = partial.shape[1]
    state = partial.reshape(ranks, rows_dev * width)
    scattered = 0
    for bit in range(bits):
        if state.shape[0] * rows_dev > 8:
            keep, send = split_rows(state, bit_of[bit])
            scattered += 1
        else:
            keep = send = state
        state = keep + swap_bit(send.astype(jnp.bfloat16), bit).astype(jnp.float32)
    state = state.reshape(-1, width)
    gain = norm_gain.astype(jnp.float32)
    normed = (
        state * lax.rsqrt(jnp.mean(state * state, axis=-1, keepdims=True) + 1e-06) * gain
    ).astype(jnp.bfloat16)
    for bit in reversed(range(scattered)):
        normed = jnp.concatenate([normed, swap_bit(normed, bit)], axis=0)
    gate = jnp.dot(normed, gate_weight, preferred_element_type=jnp.float32)
    upper = jnp.dot(normed, up_weight, preferred_element_type=jnp.float32)
    hidden = (jax.nn.silu(gate) * upper).astype(jnp.bfloat16)
    total = jnp.dot(hidden, down_weight, preferred_element_type=jnp.float32)
    for bit in range(scattered):
        keep, send = jnp.split(total, 2, axis=0)
        total = keep + swap_bit(send.astype(jnp.bfloat16), bit).astype(jnp.float32)
    total = total.reshape(-1, rows_dev * width)
    for bit in range(scattered, bits):
        keep, send = split_rows(total, bit_of[bit])
        total = keep + swap_bit(send.astype(jnp.bfloat16), bit).astype(jnp.float32)
    own = lax.dynamic_slice_in_dim(state, (rank >> scattered) * rows_dev, rows_dev, 0)
    layer_out = (own + total.reshape(rows_dev, width)).astype(jnp.bfloat16)

    held = jnp.where(flag_here[:, None, None], cache_other, cache)
    held = append_entry(held, latents[0], len_slot)
    return layer_out[None], held


def solution(mesh):
    placed = (
        P(("groups", "dp", "tp"), None, None),
        P("groups"),
        P(None, "groups"),
        P(None, ("groups", "dp", "tp"), None, None),
        P(None, ("groups", "dp", "tp"), None),
        P(None, ("groups", "dp", "tp"), None),
        P(),
        P(("dp", "tp"), None, None),
        P(("dp", "tp"), None),
        P(None, ("dp", "tp")),
        P(None, ("dp", "tp")),
        P(("dp", "tp"), None),
    )
    return jax.shard_map(
        local,
        mesh=mesh,
        in_specs=placed,
        out_specs=(P(None, ("groups", "dp", "tp"), None), P(("groups", "dp", "tp"), None, None)),
        check_vma=False,
    )
```

```python
import functools

import jax
import jax.numpy as jnp
from jax import lax
from jax.experimental import pallas as pl
from jax.experimental.pallas import tpu as pltpu
from jax.sharding import PartitionSpec as P

LATENT_WIDTH = 512
AXES = ("dp", "tp")
MIB = 1 << 20

VMEM = pl.BlockSpec(memory_space=pltpu.VMEM)
SMEM = pl.BlockSpec(memory_space=pltpu.SMEM)
ANY = pl.BlockSpec(memory_space=pl.ANY)
HBM = pl.BlockSpec(memory_space=pltpu.HBM)

FREE = pl.CostEstimate(flops=0, bytes_accessed=0, transcendentals=0)

score_scale = 0.07216878364870322


def in_vmem(array):
    return pltpu.with_memory_space_constraint(array, pltpu.VMEM)


def in_hbm(array):
    return pltpu.with_memory_space_constraint(array, pltpu.HBM)


def bytes_of(*arrays):
    return sum(array.size * array.dtype.itemsize for array in arrays)


def swap_bit(block, bit, take=lambda rank: True):
    ranks = lax.axis_size(AXES)
    route = [(rank, rank ^ 1 << bit) for rank in range(ranks) if take(rank)]
    return lax.ppermute(block, AXES, route)


def attend_kernel(
    rank, lengths_hbm, flags_hbm, query_hbm, query_other, entry_hbm, entry_other, keys_hbm,
    context, lengths, flags, query, entry, keys, sems,
):
    copies = [
        pltpu.make_async_copy(source, target, sems.at[index])
        for index, (source, target) in enumerate(
            [
                (lengths_hbm, lengths),
                (flags_hbm, flags),
                (query_hbm, query),
                (entry_hbm, entry),
                (keys_hbm, keys),
            ]
        )
    ]
    for copy in copies:
        copy.start()
    for copy in copies[:4]:
        copy.wait()
    slot = rank[0]
    live = lengths[slot]
    swapped = flags[0, slot] == 1
    new_wide = jnp.where(
        swapped, entry_other[...].astype(jnp.float32), entry[...].astype(jnp.float32)
    )
    rows = jnp.where(swapped, query_other[...], query[...]).T
    new_score = jnp.sum(rows.astype(jnp.float32) * new_wide, axis=1, keepdims=True)
    copies[4].wait()
    keys_now = keys[...]
    scores = jnp.dot(rows, keys_now, preferred_element_type=jnp.float32)
    positions = lax.broadcasted_iota(jnp.int32, scores.shape, 1)
    scores = jnp.where(positions == live, new_score, scores) * score_scale
    scores = jnp.where(positions <= live, scores, -1e30)
    top = jnp.max(scores, axis=1, keepdims=True)
    weights = jnp.where(positions <= live, jnp.exp(scores - top), 0.0)
    total = jnp.sum(weights, axis=1, keepdims=True)
    probs = (weights / total).astype(jnp.bfloat16)
    new_prob = (jnp.exp(new_score * score_scale - top) / total).astype(jnp.bfloat16)
    probs = jnp.where(positions == live, jnp.zeros_like(probs), probs)
    result = lax.dot_general(
        probs,
        keys_now[:LATENT_WIDTH],
        (((1,), (1,)), ((), ())),
        preferred_element_type=jnp.float32,
    )
    result = result + new_prob.astype(jnp.float32) * new_wide[:, :LATENT_WIDTH]
    context[...] = result.astype(jnp.bfloat16)


def attend(rank, lengths, flags, query, query_other, entry, entry_other, keys):
    heads = query.shape[1]
    return pl.pallas_call(
        attend_kernel,
        out_shape=jax.ShapeDtypeStruct((heads, LATENT_WIDTH), jnp.bfloat16),
        in_specs=[SMEM, HBM, HBM, HBM, VMEM, HBM, VMEM, HBM],
        out_specs=VMEM,
        scratch_shapes=[
            pltpu.SMEM(lengths.shape, lengths.dtype),
            pltpu.SMEM(flags.shape, flags.dtype),
            pltpu.VMEM(query.shape, query.dtype),
            pltpu.VMEM(entry.shape, entry.dtype),
            pltpu.VMEM(keys.shape, keys.dtype),
            pltpu.SemaphoreType.DMA((5,)),
        ],
        compiler_params=pltpu.CompilerParams(vmem_limit_bytes=12 * MIB),
        cost_estimate=FREE,
        name="attend",
    )(
        rank,
        in_hbm(lengths),
        in_hbm(flags),
        in_hbm(query),
        query_other,
        in_hbm(entry),
        entry_other,
        in_hbm(keys),
    )


def project_kernel(
    rank, flags_hbm, per_head, expand_hbm, residual_hbm, weight,
    keep, send, flags, expand, residual, weight_here, values_here, sems, small_sems,
):
    rows, heads, _ = per_head.shape
    half = rows // 2
    small = [
        pltpu.make_async_copy(source, target, small_sems.at[index])
        for index, (source, target) in enumerate(
            [(flags_hbm, flags), (expand_hbm, expand), (residual_hbm, residual)]
        )
    ]
    chunks, chunk = chunks_of(weight.shape[1])
    copies = [
        pltpu.make_async_copy(weight.at[:, columns], weight_here.at[:, columns], sems.at[index])
        for index, columns in enumerate(pl.ds(i * chunk, chunk) for i in range(chunks))
    ]
    for copy in small + copies:
        copy.start()
    for copy in small:
        copy.wait()
    bit = rank[0] % 2
    place = lax.broadcasted_iota(jnp.int32, (rows, 1), 0)
    source = jnp.zeros((rows, 1), jnp.int32)
    for position in range(rows):
        slot = 2 * position + bit if position < half else 2 * (position - half) + 1 - bit
        row = jnp.where(flags[0, slot] == 1, (slot + half) % rows, slot)
        source = jnp.where(place == position, row, source)
    pick = (lax.broadcasted_iota(jnp.int32, (rows, rows), 1) == source).astype(jnp.bfloat16)
    values = [
        jnp.dot(per_head[:, head, :], expand[head], preferred_element_type=jnp.float32).astype(
            jnp.bfloat16
        )
        for head in range(heads)
    ]
    values = values[0] if heads == 1 else jnp.concatenate(values, axis=1)
    values_here[...] = jnp.dot(pick, values, preferred_element_type=jnp.float32).astype(
        jnp.bfloat16
    )
    mine = lax.broadcasted_iota(jnp.int32, (half, 1), 0) == rank[0] // 2

    @pl.loop(0, chunks)
    def _(index):
        columns = pl.ds(pl.multiple_of(index * chunk, chunk), chunk)
        pltpu.make_async_copy(
            weight.at[:, columns], weight_here.at[:, columns], sems.at[index]
        ).wait()
        partial = jnp.dot(
            values_here[...], weight_here[:, columns], preferred_element_type=jnp.float32
        )
        own = residual[:, columns].astype(jnp.float32)
        keep[:, columns] = partial[:half] + jnp.where(mine, own, 0.0)
        send[:, columns] = partial[half:].astype(jnp.bfloat16)


def chunks_of(size, most=1024):
    chunk = most
    while size % chunk:
        chunk //= 2
    return size // chunk, chunk


def project(rank, flags, per_head, expand, weight, residual):
    rows, (depth, width) = per_head.shape[0], weight.shape
    half = rows // 2
    return pl.pallas_call(
        project_kernel,
        out_shape=(
            jax.ShapeDtypeStruct((half, width), jnp.float32),
            jax.ShapeDtypeStruct((half, width), jnp.bfloat16),
        ),
        in_specs=[SMEM, HBM, VMEM, HBM, HBM, HBM],
        out_specs=(VMEM, VMEM),
        scratch_shapes=[
            pltpu.SMEM(flags.shape, flags.dtype),
            pltpu.VMEM(expand.shape, expand.dtype),
            pltpu.VMEM(residual.shape, residual.dtype),
            pltpu.VMEM(weight.shape, weight.dtype),
            pltpu.VMEM((rows, depth), jnp.bfloat16),
            pltpu.SemaphoreType.DMA((chunks_of(width)[0],)),
            pltpu.SemaphoreType.DMA((3,)),
        ],
        compiler_params=pltpu.CompilerParams(vmem_limit_bytes=bytes_of(weight) + 10 * MIB),
        cost_estimate=FREE,
        name="project",
    )(
        rank, in_hbm(flags), per_head, in_hbm(expand), in_hbm(residual), in_hbm(weight)
    )


def add_kernel(keep, arrived, total, send):
    result = keep[...] + arrived[...].astype(jnp.float32)
    total[...] = result
    send[...] = result.astype(send.dtype)


def add(keep, arrived):
    return pl.pallas_call(
        add_kernel,
        out_shape=(
            jax.ShapeDtypeStruct(keep.shape, jnp.float32),
            jax.ShapeDtypeStruct(keep.shape, jnp.bfloat16),
        ),
        in_specs=[VMEM, VMEM],
        out_specs=(VMEM, VMEM),
        compiler_params=pltpu.CompilerParams(vmem_limit_bytes=8 * MIB),
        cost_estimate=FREE,
        name="add",
    )(keep, arrived)


def norm_kernel(rank, keep, arrived, gain, normed, own):
    state = keep[...] + arrived[...].astype(jnp.float32)
    scale = lax.rsqrt(jnp.mean(state * state, axis=1, keepdims=True) + 1e-06)
    normed[...] = (state * scale * gain[...].astype(jnp.float32)).astype(normed.dtype)
    place = lax.broadcasted_iota(jnp.int32, (state.shape[0], 1), 0)
    own[...] = jnp.sum(
        jnp.where(place == rank[0] // 2, state, 0.0), axis=0, keepdims=True
    )


def norm(rank, keep, arrived, gain):
    return pl.pallas_call(
        norm_kernel,
        out_shape=(
            jax.ShapeDtypeStruct(keep.shape, jnp.bfloat16),
            jax.ShapeDtypeStruct((1, keep.shape[1]), jnp.float32),
        ),
        in_specs=[SMEM, VMEM, VMEM, VMEM],
        out_specs=(VMEM, VMEM),
        compiler_params=pltpu.CompilerParams(vmem_limit_bytes=8 * MIB),
        cost_estimate=FREE,
        name="norm",
    )(rank, keep, arrived, gain.reshape(1, -1))


DEPTH = 512


def feed_kernel(
    rank, mine, other, gate, up, down, keep, send, rows_here, gate_here, up_here, down_here,
    hidden_here, gate_sems, up_sems, down_sems,
):
    half = mine.shape[0]
    rows = 2 * half
    steps = gate.shape[0] // DEPTH
    chunks, chunk = chunks_of(down.shape[1])

    def part(index, size):
        if isinstance(index, int):
            return pl.ds(index * size, size)
        return pl.ds(pl.multiple_of(index * size, size), size)

    def gate_copy(index):
        here = part(index, DEPTH)
        return pltpu.make_async_copy(gate.at[here], gate_here.at[here], gate_sems.at[index])

    def up_copy(index):
        here = part(index, DEPTH)
        return pltpu.make_async_copy(up.at[here], up_here.at[here], up_sems.at[index])

    def down_copy(index):
        here = part(index, chunk)
        return pltpu.make_async_copy(down.at[:, here], down_here.at[:, here], down_sems.at[index])

    for index in range(steps):
        gate_copy(index).start()
        up_copy(index).start()
    for index in range(chunks):
        down_copy(index).start()
    rows_here[...] = jnp.concatenate(
        [mine[...].astype(jnp.float32), other[...].astype(jnp.float32)], axis=0
    ).astype(jnp.bfloat16)

    def step(index, total):
        here = part(index, DEPTH)
        block = rows_here[:, here]
        gate_copy(index).wait()
        gated = total[0] + jnp.dot(block, gate_here[here], preferred_element_type=jnp.float32)
        up_copy(index).wait()
        upper = total[1] + jnp.dot(block, up_here[here], preferred_element_type=jnp.float32)
        return gated, upper

    zeros = jnp.zeros((rows, gate.shape[1]), jnp.float32)
    gated, upper = lax.fori_loop(0, steps, step, (zeros, zeros))
    hidden = (gated * jax.nn.sigmoid(gated) * upper).astype(jnp.bfloat16)

    free = rows.bit_length() - 2
    place = lax.broadcasted_iota(jnp.int32, (rows, 1), 0)
    source = jnp.zeros((rows, 1), jnp.int32)
    for position in range(rows):
        inner = position % half
        mirrored = sum(((inner >> bit) & 1) << (free - 1 - bit) for bit in range(free))
        row = position - inner + ((rank[0] // 2) ^ mirrored)
        source = jnp.where(place == position, row, source)
    pick = (lax.broadcasted_iota(jnp.int32, (rows, rows), 1) == source).astype(jnp.bfloat16)
    hidden_here[...] = jnp.dot(pick, hidden, preferred_element_type=jnp.float32).astype(
        jnp.bfloat16
    )

    @pl.loop(0, chunks)
    def _(index):
        here = part(index, chunk)
        down_copy(index).wait()
        total = jnp.dot(hidden_here[...], down_here[:, here], preferred_element_type=jnp.float32)
        keep[:, here] = total[:half]
        send[:, here] = total[half:].astype(jnp.bfloat16)


def feed(rank, mine, other, gate, up, down):
    half, width = mine.shape[0], down.shape[1]
    steps = gate.shape[0] // DEPTH
    return pl.pallas_call(
        feed_kernel,
        out_shape=(
            jax.ShapeDtypeStruct((half, width), jnp.float32),
            jax.ShapeDtypeStruct((half, width), jnp.bfloat16),
        ),
        in_specs=[SMEM, VMEM, VMEM, HBM, HBM, HBM],
        out_specs=(VMEM, VMEM),
        scratch_shapes=[
            pltpu.VMEM((2 * half, mine.shape[1]), jnp.bfloat16),
            pltpu.VMEM(gate.shape, gate.dtype),
            pltpu.VMEM(up.shape, up.dtype),
            pltpu.VMEM(down.shape, down.dtype),
            pltpu.VMEM((2 * half, down.shape[0]), jnp.bfloat16),
            pltpu.SemaphoreType.DMA((steps,)),
            pltpu.SemaphoreType.DMA((steps,)),
            pltpu.SemaphoreType.DMA((chunks_of(width)[0],)),
        ],
        compiler_params=pltpu.CompilerParams(vmem_limit_bytes=bytes_of(gate, up, down) + 6 * MIB),
        cost_estimate=FREE,
        name="feed",
    )(rank, mine, other, in_hbm(gate), in_hbm(up), in_hbm(down))


def hold_kernel(rank, lengths, flags, entry, own, arrived, held, block, sems):
    slot = rank[0]
    ranks = lengths.shape[0]
    swapped = flags[0, slot] == 1
    position = lengths[jnp.where(swapped, (slot + ranks // 2) % ranks, slot)]

    @pl.when(swapped)
    def _():
        copy = pltpu.make_async_copy(arrived, block, sems.at[0])
        copy.start()
        copy.wait()

    @pl.when(jnp.logical_not(swapped))
    def _():
        copy = pltpu.make_async_copy(own, block, sems.at[1])
        copy.start()
        copy.wait()

    column = entry[...].astype(jnp.float32).T.astype(block.dtype)
    tile = position // 128
    here = pl.ds(pl.multiple_of(tile * 128, 128), 128)
    lanes = lax.broadcasted_iota(jnp.int32, (block.shape[0], 128), 1)
    block[:, here] = jnp.where(lanes == position - tile * 128, column, block[:, here])
    store = pltpu.make_async_copy(block, held, sems.at[2])
    store.start()
    store.wait()


def hold(rank, lengths, flags, entry, own, arrived):
    return pl.pallas_call(
        hold_kernel,
        out_shape=jax.ShapeDtypeStruct(own.shape, own.dtype),
        in_specs=[SMEM, SMEM, SMEM, VMEM, HBM, HBM],
        out_specs=ANY,
        scratch_shapes=[pltpu.VMEM(own.shape, own.dtype), pltpu.SemaphoreType.DMA((3,))],
        compiler_params=pltpu.CompilerParams(vmem_limit_bytes=6 * MIB),
        cost_estimate=FREE,
        name="hold",
    )(rank, lengths, flags, entry, in_hbm(own), in_hbm(arrived))


def local(
    cache,
    lengths,
    swap_flags,
    queries,
    latents,
    residual,
    norm_gain,
    value_expand_weight,
    out_proj,
    gate_weight,
    up_weight,
    down_weight,
):
    ranks = lax.axis_size(AXES)
    bits = ranks.bit_length() - 1
    top = bits - 1
    rank = lax.axis_index(AXES)
    here = rank.reshape(1)
    keys = jnp.swapaxes(cache[0], 0, 1)
    query = jnp.swapaxes(queries[0, 0], 0, 1)
    entry = latents[0]

    query_other = swap_bit(query, top)
    entry_other = swap_bit(entry, top)
    context = attend(here, lengths, swap_flags, query, query_other, entry, entry_other, keys)

    heads = context.shape[0] // ranks
    per_head = lax.all_to_all(
        context.reshape(ranks, heads, LATENT_WIDTH), AXES, split_axis=0, concat_axis=0, tiled=True
    )
    keep, send = project(here, swap_flags, per_head, value_expand_weight, out_proj, residual[0])

    keep, send = add(keep, swap_bit(send, 0))
    for bit in range(2, bits):
        keep, send = add(keep, swap_bit(send, bit))

    def near(keep, send):
        normed, own = norm(here, keep, swap_bit(send, 1), norm_gain)
        keep, send = feed(here, normed, swap_bit(normed, 0), gate_weight, up_weight, down_weight)
        total = keep + swap_bit(send, 0).astype(jnp.float32)
        keep, send = jnp.split(total, 2, axis=0)
        total = keep + swap_bit(send.astype(jnp.bfloat16), 1).astype(jnp.float32)
        return total, own

    def beside(movers):
        def branch(keep, send):
            if not movers:
                return *near(keep, send), jnp.zeros_like(keys)
            arrived = swap_bit(keys, top, lambda rank: movers >> rank % 4 & 1)
            some = (jnp.zeros((keep.shape[0] // 2, width), jnp.float32), residual[0].astype(jnp.float32))
            total, own = lax.cond(lengths[0] > 0, near, lambda *_: some, keep, send)
            arrived, _ = lax.optimization_barrier((arrived, total))
            return total, own, arrived

        return branch

    width = keep.shape[1]
    first = rank // 4 * 4
    movers = sum(swap_flags[0, first + each] << each for each in range(4))
    total, own, arrived = lax.switch(movers, [beside(movers) for movers in range(16)], keep, send)

    for bit in range(2, bits):
        keep, send = jnp.split(total, 2, axis=0)
        total = keep + swap_bit(send.astype(jnp.bfloat16), bit).astype(jnp.float32)
    layer_out = (own + total).astype(jnp.bfloat16)
    held = hold(here, lengths, swap_flags, entry, keys, arrived)
    return layer_out[None], jnp.swapaxes(held, 0, 1)[None]


def solution(mesh):
    placed = (
        P(("groups", "dp", "tp"), None, None),
        P("groups"),
        P(None, "groups"),
        P(None, ("groups", "dp", "tp"), None, None),
        P(None, ("groups", "dp", "tp"), None),
        P(None, ("groups", "dp", "tp"), None),
        P(),
        P(("dp", "tp"), None, None),
        P(("dp", "tp"), None),
        P(None, ("dp", "tp")),
        P(None, ("dp", "tp")),
        P(("dp", "tp"), None),
    )
    return jax.shard_map(
        local,
        mesh=mesh,
        in_specs=placed,
        out_specs=(P(None, ("groups", "dp", "tp"), None), P(("groups", "dp", "tp"), None, None)),
        check_vma=False,
    )
```

```python
import functools

import jax
import jax.numpy as jnp
from jax import lax
from jax.experimental import pallas as pl
from jax.experimental.pallas import tpu as pltpu
from jax.sharding import PartitionSpec as P

LATENT_WIDTH = 512
AXES = ("dp", "tp")
MIB = 1 << 20

VMEM = pl.BlockSpec(memory_space=pltpu.VMEM)
SMEM = pl.BlockSpec(memory_space=pltpu.SMEM)
ANY = pl.BlockSpec(memory_space=pl.ANY)
HBM = pl.BlockSpec(memory_space=pltpu.HBM)

FREE = pl.CostEstimate(flops=0, bytes_accessed=0, transcendentals=0)

LONG = pl.CostEstimate(flops=10**12, bytes_accessed=10**9, transcendentals=0)

score_scale = 0.07216878364870322


def in_vmem(array):
    return pltpu.with_memory_space_constraint(array, pltpu.VMEM)


def in_hbm(array):
    return pltpu.with_memory_space_constraint(array, pltpu.HBM)


def bytes_of(*arrays):
    return sum(array.size * array.dtype.itemsize for array in arrays)


def swap_bit(block, bit, take=lambda rank: True):
    ranks = lax.axis_size(AXES)
    route = [(rank, rank ^ 1 << bit) for rank in range(ranks) if take(rank)]
    return lax.ppermute(block, AXES, route)


def attend_kernel(
    rank, lengths_hbm, flags_hbm, query_hbm, query_other, entry_hbm, entry_other, keys,
    context, lengths, flags, query, entry, sems,
):
    copies = [
        pltpu.make_async_copy(source, target, sems.at[index])
        for index, (source, target) in enumerate(
            [
                (lengths_hbm, lengths),
                (flags_hbm, flags),
                (query_hbm, query),
                (entry_hbm, entry),
            ]
        )
    ]
    for copy in copies:
        copy.start()
    for copy in copies:
        copy.wait()
    slot = rank[0]
    live = lengths[slot]
    swapped = flags[0, slot] == 1
    new_wide = jnp.where(
        swapped, entry_other[...].astype(jnp.float32), entry[...].astype(jnp.float32)
    )
    rows = jnp.where(swapped, query_other[...], query[...]).T
    new_score = jnp.sum(rows.astype(jnp.float32) * new_wide, axis=1, keepdims=True)
    keys_now = keys[...]
    scores = jnp.dot(rows, keys_now, preferred_element_type=jnp.float32)
    positions = lax.broadcasted_iota(jnp.int32, scores.shape, 1)
    scores = jnp.where(positions == live, new_score, scores) * score_scale
    scores = jnp.where(positions <= live, scores, -1e30)
    top = jnp.max(scores, axis=1, keepdims=True)
    weights = jnp.where(positions <= live, jnp.exp(scores - top), 0.0)
    total = jnp.sum(weights, axis=1, keepdims=True)
    probs = (weights / total).astype(jnp.bfloat16)
    new_prob = (jnp.exp(new_score * score_scale - top) / total).astype(jnp.bfloat16)
    probs = jnp.where(positions == live, jnp.zeros_like(probs), probs)
    result = lax.dot_general(
        probs,
        keys_now[:LATENT_WIDTH],
        (((1,), (1,)), ((), ())),
        preferred_element_type=jnp.float32,
    )
    result = result + new_prob.astype(jnp.float32) * new_wide[:, :LATENT_WIDTH]
    context[...] = result.astype(jnp.bfloat16)


def attend(rank, lengths, flags, query, query_other, entry, entry_other, keys):
    heads = query.shape[1]
    return pl.pallas_call(
        attend_kernel,
        out_shape=jax.ShapeDtypeStruct((heads, LATENT_WIDTH), jnp.bfloat16),
        in_specs=[SMEM, HBM, HBM, HBM, VMEM, HBM, VMEM, VMEM],
        out_specs=VMEM,
        scratch_shapes=[
            pltpu.SMEM(lengths.shape, lengths.dtype),
            pltpu.SMEM(flags.shape, flags.dtype),
            pltpu.VMEM(query.shape, query.dtype),
            pltpu.VMEM(entry.shape, entry.dtype),
            pltpu.SemaphoreType.DMA((4,)),
        ],
        compiler_params=pltpu.CompilerParams(vmem_limit_bytes=12 * MIB),
        cost_estimate=FREE,
        name="attend",
    )(
        rank,
        in_hbm(lengths),
        in_hbm(flags),
        in_hbm(query),
        query_other,
        in_hbm(entry),
        entry_other,
        in_vmem(keys),
    )


def project_kernel(
    rank, flags_hbm, per_head, expand_hbm, residual_hbm, weight,
    keep, send, flags, expand, residual, weight_here, values_here, sems, small_sems,
):
    heads, _, width = expand.shape
    rows = per_head.shape[0] // heads
    half = rows // 2
    small = [
        pltpu.make_async_copy(source, target, small_sems.at[index])
        for index, (source, target) in enumerate(
            [(flags_hbm, flags), (expand_hbm, expand), (residual_hbm, residual)]
        )
    ]
    parts = parts_of(weight.shape[1])
    copies = [
        pltpu.make_async_copy(weight.at[:, part], weight_here.at[:, part], sems.at[index])
        for index, part in enumerate(parts)
    ]
    for copy in small + copies:
        copy.start()
    for copy in small:
        copy.wait()
    bit = rank[0] % 2
    place = lax.broadcasted_iota(jnp.int32, (rows, 1), 0)
    source = jnp.zeros((rows, 1), jnp.int32)
    for position in range(rows):
        slot = 2 * position + bit if position < half else 2 * (position - half) + 1 - bit
        row = jnp.where(flags[0, slot] == 1, (slot + half) % rows, slot)
        source = jnp.where(place == position, row, source)
    lanes = lax.broadcasted_iota(jnp.int32, (rows, rows * heads), 1)
    for head in range(heads):
        pick = (lanes == source * heads + head).astype(jnp.bfloat16)
        latent = jnp.dot(pick, per_head[...], preferred_element_type=jnp.float32)
        values_here[:, head * width : (head + 1) * width] = jnp.dot(
            latent.astype(jnp.bfloat16), expand[head], preferred_element_type=jnp.float32
        ).astype(jnp.bfloat16)
    mine = lax.broadcasted_iota(jnp.int32, (half, 1), 0) == rank[0] // 2

    for copy, part in zip(copies, parts):
        copy.wait()
        partial = jnp.dot(
            values_here[...], weight_here[:, part], preferred_element_type=jnp.float32
        )
        own = residual[:, part].astype(jnp.float32)
        keep[:, part] = partial[:half] + jnp.where(mine, own, 0.0)
        send[:, part] = partial[half:].astype(jnp.bfloat16)


def each_part(size, count, body):
    part = size // count

    @pl.loop(0, count)
    def _(index):
        body(index, pl.ds(pl.multiple_of(index * part, part), part))


def parts_of(size):
    cuts = [0, size // 2, size * 6 // 7, size]
    return [pl.ds(low, high - low) for low, high in zip(cuts, cuts[1:])]


def project(rank, flags, per_head, expand, weight, residual):
    rows, (depth, width) = per_head.shape[0] // expand.shape[0], weight.shape
    half = rows // 2
    return pl.pallas_call(
        project_kernel,
        out_shape=(
            jax.ShapeDtypeStruct((half, width), jnp.float32),
            jax.ShapeDtypeStruct((half, width), jnp.bfloat16),
        ),
        in_specs=[SMEM, HBM, VMEM, HBM, HBM, HBM],
        out_specs=(VMEM, VMEM),
        scratch_shapes=[
            pltpu.SMEM(flags.shape, flags.dtype),
            pltpu.VMEM(expand.shape, expand.dtype),
            pltpu.VMEM(residual.shape, residual.dtype),
            pltpu.VMEM(weight.shape, weight.dtype),
            pltpu.VMEM((rows, depth), jnp.bfloat16),
            pltpu.SemaphoreType.DMA((len(parts_of(width)),)),
            pltpu.SemaphoreType.DMA((3,)),
        ],
        compiler_params=pltpu.CompilerParams(vmem_limit_bytes=bytes_of(weight) + 10 * MIB),
        cost_estimate=FREE,
        name="project",
    )(
        rank, in_hbm(flags), per_head, in_hbm(expand), in_hbm(residual), in_hbm(weight)
    )


def add_kernel(keep, arrived, total, send):
    def body(index, here):
        result = keep[:, here] + arrived[:, here].astype(jnp.float32)
        total[:, here] = result
        send[:, here] = result.astype(send.dtype)

    each_part(keep.shape[1], 7, body)


def add(keep, arrived):
    return pl.pallas_call(
        add_kernel,
        out_shape=(
            jax.ShapeDtypeStruct(keep.shape, jnp.float32),
            jax.ShapeDtypeStruct(keep.shape, jnp.bfloat16),
        ),
        in_specs=[VMEM, VMEM],
        out_specs=(VMEM, VMEM),
        compiler_params=pltpu.CompilerParams(vmem_limit_bytes=8 * MIB),
        cost_estimate=FREE,
        name="add",
    )(keep, arrived)


def halve_kernel(keep, arrived, kept, send):
    half = keep.shape[0] // 2

    def body(index, here):
        total = keep[:, here] + arrived[:, here].astype(jnp.float32)
        kept[:, here] = total[:half]
        send[:, here] = total[half:].astype(send.dtype)

    each_part(keep.shape[1], 7, body)


def halve(keep, arrived, cost=FREE):
    shape = (keep.shape[0] // 2, keep.shape[1])
    return pl.pallas_call(
        halve_kernel,
        out_shape=(
            jax.ShapeDtypeStruct(shape, jnp.float32),
            jax.ShapeDtypeStruct(shape, jnp.bfloat16),
        ),
        in_specs=[VMEM, VMEM],
        out_specs=(VMEM, VMEM),
        compiler_params=pltpu.CompilerParams(vmem_limit_bytes=8 * MIB),
        cost_estimate=cost,
        name="halve",
    )(keep, arrived)


def finish_kernel(keep, arrived, out):
    out[...] = (keep[...] + arrived[...].astype(jnp.float32)).astype(out.dtype)


def finish(keep, arrived):
    return pl.pallas_call(
        finish_kernel,
        out_shape=jax.ShapeDtypeStruct(keep.shape, jnp.bfloat16),
        in_specs=[VMEM, VMEM],
        out_specs=VMEM,
        compiler_params=pltpu.CompilerParams(vmem_limit_bytes=8 * MIB),
        cost_estimate=FREE,
        name="finish",
    )(keep, arrived)


def load_kernel(source, after, target, sem):
    copy = pltpu.make_async_copy(source.at[pl.ds(0, target.shape[0])], target, sem)
    copy.start()
    copy.wait()


def load(array, rows, after):
    return pl.pallas_call(
        load_kernel,
        out_shape=pltpu.VMEM((rows, array.shape[1]), array.dtype),
        in_specs=[HBM, ANY],
        out_specs=VMEM,
        scratch_shapes=[pltpu.SemaphoreType.DMA],
        compiler_params=pltpu.CompilerParams(vmem_limit_bytes=MIB),
        cost_estimate=FREE,
        name="load_weight",
    )(in_hbm(array), after)


def norm_kernel(rank, keep, arrived, gain, normed, own, square):
    rows, width = keep.shape
    mine = lax.broadcasted_iota(jnp.int32, (rows, 1), 0) == rank[0] // 2
    square[...] = jnp.zeros_like(square)

    def measure(index, here):
        state = keep[:, here] + arrived[:, here].astype(jnp.float32)
        square[...] += jnp.sum(state * state, axis=1, keepdims=True)
        own[:, here] = jnp.sum(jnp.where(mine, state, 0.0), axis=0, keepdims=True)

    each_part(width, 7, measure)
    scale = lax.rsqrt(square[...] / width + 1e-06)

    def rescale(index, here):
        state = keep[:, here] + arrived[:, here].astype(jnp.float32)
        normed[:, here] = (state * scale * gain[:, here].astype(jnp.float32)).astype(normed.dtype)

    each_part(width, 7, rescale)


def norm(rank, keep, arrived, gain):
    return pl.pallas_call(
        norm_kernel,
        out_shape=(
            jax.ShapeDtypeStruct(keep.shape, jnp.bfloat16),
            jax.ShapeDtypeStruct((1, keep.shape[1]), jnp.float32),
        ),
        in_specs=[SMEM, VMEM, VMEM, VMEM],
        out_specs=(VMEM, VMEM),
        scratch_shapes=[pltpu.VMEM((keep.shape[0], 1), jnp.float32)],
        compiler_params=pltpu.CompilerParams(vmem_limit_bytes=8 * MIB),
        cost_estimate=FREE,
        name="norm",
    )(rank, keep, arrived, gain.reshape(1, -1))


DEPTH = 512
PARTS = 4


def feed_kernel(
    order, rank, mine, other, own, gate_low, gate, up, down, keep, send, rows_here, gate_here,
    up_here, down_here, hidden_here, gate_sems, up_sems, down_sems,
):
    half = mine.shape[0]
    rows = 2 * half
    steps, low = gate.shape[0] // DEPTH, gate_low.shape[0] // DEPTH
    width = down.shape[1]
    part = width // PARTS

    def depth(index):
        return pl.ds(pl.multiple_of(index * DEPTH, DEPTH), DEPTH)

    def gate_copy(index):
        source, target = gate.at[depth(index)], gate_here.at[depth(index - low)]
        return pltpu.make_async_copy(source, target, gate_sems.at[index])

    def up_copy(index):
        source, target = up.at[depth(index)], up_here.at[depth(index)]
        return pltpu.make_async_copy(source, target, up_sems.at[index])

    def down_copy(index, here):
        return pltpu.make_async_copy(down.at[:, here], down_here.at[:, here], down_sems.at[index])

    for index in range(steps):
        if index >= low:
            gate_copy(index).start()
        up_copy(index).start()
    for index in range(PARTS):
        down_copy(index, pl.ds(index * part, part)).start()

    def place_rows(index, here):
        rows_here[:, here] = jnp.concatenate(
            [mine[:, here].astype(jnp.float32), other[:, here].astype(jnp.float32)], axis=0
        ).astype(jnp.bfloat16)

    each_part(mine.shape[1], 7, place_rows)


    def step(index, total, gate_part):
        block = rows_here[:, depth(index)]
        gated = total[0] + jnp.dot(block, gate_part, preferred_element_type=jnp.float32)
        up_copy(index).wait()
        up_part = up_here[depth(index)]
        return gated, total[1] + jnp.dot(block, up_part, preferred_element_type=jnp.float32)

    def low_step(index, total):
        return step(index, total, gate_low[depth(index)])

    def high_step(index, total):
        gate_copy(index).wait()
        return step(index, total, gate_here[depth(index - low)])

    zeros = jnp.zeros((rows, gate.shape[1]), jnp.float32)
    total = lax.fori_loop(0, low, low_step, (zeros, zeros))
    gated, upper = lax.fori_loop(low, steps, high_step, total)
    hidden = (gated * jax.nn.sigmoid(gated) * upper).astype(jnp.bfloat16)

    place = lax.broadcasted_iota(jnp.int32, (rows, 1), 0)
    source = jnp.zeros((rows, 1), jnp.int32)
    for position in range(rows):
        inner = position % half
        other_bits = sum(
            (inner >> len(order) - 1 - index & 1) << bit - 1 for index, bit in enumerate(order)
        )
        row = position - inner + ((rank[0] // 2) ^ other_bits)
        source = jnp.where(place == position, row, source)
    pick = (lax.broadcasted_iota(jnp.int32, (rows, rows), 1) == source).astype(jnp.bfloat16)
    hidden_here[...] = jnp.dot(pick, hidden, preferred_element_type=jnp.float32).astype(
        jnp.bfloat16
    )

    first = lax.broadcasted_iota(jnp.int32, (half, 1), 0) == 0

    def project_down(index, here):
        down_copy(index, here).wait()
        total = jnp.dot(hidden_here[...], down_here[:, here], preferred_element_type=jnp.float32)
        keep[:, here] = total[:half] + jnp.where(first, own[:, here], 0.0)
        send[:, here] = total[half:].astype(jnp.bfloat16)

    each_part(width, PARTS, project_down)


def feed(order, rank, mine, other, own, gate_low, gate, up, down):
    half, width = mine.shape[0], down.shape[1]
    steps = gate.shape[0] // DEPTH
    return pl.pallas_call(
        functools.partial(feed_kernel, order),
        out_shape=(
            jax.ShapeDtypeStruct((half, width), jnp.float32),
            jax.ShapeDtypeStruct((half, width), jnp.bfloat16),
        ),
        in_specs=[SMEM, VMEM, VMEM, VMEM, VMEM, HBM, HBM, HBM],
        out_specs=(VMEM, VMEM),
        scratch_shapes=[
            pltpu.VMEM((2 * half, mine.shape[1]), jnp.bfloat16),
            pltpu.VMEM((gate.shape[0] - gate_low.shape[0], gate.shape[1]), gate.dtype),
            pltpu.VMEM(up.shape, up.dtype),
            pltpu.VMEM(down.shape, down.dtype),
            pltpu.VMEM((2 * half, down.shape[0]), jnp.bfloat16),
            pltpu.SemaphoreType.DMA((steps,)),
            pltpu.SemaphoreType.DMA((steps,)),
            pltpu.SemaphoreType.DMA((PARTS,)),
        ],
        compiler_params=pltpu.CompilerParams(
            vmem_limit_bytes=bytes_of(gate, up, down) - bytes_of(gate_low) + 6 * MIB
        ),
        cost_estimate=FREE,
        name="feed",
    )(
        rank, mine, other, own, in_vmem(gate_low), in_hbm(gate), in_hbm(up), in_hbm(down)
    )


def hold_kernel(
    rank, lengths, flags, entry, own, arrived, held, block, fetched, stored
):
    slot = rank[0]
    ranks = lengths.shape[0]
    swapped = flags[0, slot] == 1
    position = lengths[jnp.where(swapped, (slot + ranks // 2) % ranks, slot)]

    parts = [pl.ds(low, own.shape[0] // 4) for low in range(0, own.shape[0], own.shape[0] // 4)]

    def fetch(source):
        for index, part in enumerate(parts):
            pltpu.make_async_copy(source.at[part], block.at[part], fetched.at[index]).start()

    @pl.when(swapped)
    def _():
        fetch(arrived)

    @pl.when(jnp.logical_not(swapped))
    def _():
        fetch(own)

    column = entry[...].astype(jnp.float32).T.astype(block.dtype)
    tile = position // 128
    here = pl.ds(pl.multiple_of(tile * 128, 128), 128)
    lanes = lax.broadcasted_iota(jnp.int32, (own.shape[0] // 4, 128), 1)
    stores = []
    for index, part in enumerate(parts):
        pltpu.make_async_copy(own.at[part], block.at[part], fetched.at[index]).wait()
        column_part = column[part.start : part.start + part.size]
        block[part, here] = jnp.where(lanes == position - tile * 128, column_part, block[part, here])
        store = pltpu.make_async_copy(block.at[part], held.at[part], stored.at[index])
        store.start()
        stores.append(store)
    for store in stores:
        store.wait()


def hold(rank, lengths, flags, entry, own, arrived):
    return pl.pallas_call(
        hold_kernel,
        out_shape=jax.ShapeDtypeStruct(own.shape, own.dtype),
        in_specs=[SMEM, SMEM, SMEM, VMEM, HBM, HBM],
        out_specs=ANY,
        scratch_shapes=[
            pltpu.VMEM(own.shape, own.dtype),
            pltpu.SemaphoreType.DMA((4,)),
            pltpu.SemaphoreType.DMA((4,)),
        ],
        compiler_params=pltpu.CompilerParams(vmem_limit_bytes=6 * MIB),
        cost_estimate=FREE,
        name="hold",
    )(rank, lengths, flags, entry, in_hbm(own), in_hbm(arrived))


def local(
    cache,
    lengths,
    swap_flags,
    queries,
    latents,
    residual,
    norm_gain,
    value_expand_weight,
    out_proj,
    gate_weight,
    up_weight,
    down_weight,
):
    ranks = lax.axis_size(AXES)
    bits = ranks.bit_length() - 1
    top = bits - 1
    rank = lax.axis_index(AXES)
    here = rank.reshape(1)
    keys = jnp.swapaxes(cache[0], 0, 1)
    query = jnp.swapaxes(queries[0, 0], 0, 1)
    entry = latents[0]

    query_other = swap_bit(query, top)
    entry_other = swap_bit(entry, top)
    first = rank // 4 * 4
    movers = sum(swap_flags[0, first + each] << each for each in range(4))
    keys_here = load(keys, keys.shape[0], entry)
    query_other, keys_here, movers = lax.optimization_barrier((query_other, keys_here, movers))
    context = attend(here, lengths, swap_flags, query, query_other, entry, entry_other, keys_here)

    heads = context.shape[0] // ranks
    per_head = lax.all_to_all(
        context.reshape(ranks, heads, LATENT_WIDTH), AXES, split_axis=0, concat_axis=0, tiled=True
    ).reshape(ranks * heads, LATENT_WIDTH)
    keep, send = project(here, swap_flags, per_head, value_expand_weight, out_proj, residual[0])

    keep, send = add(keep, swap_bit(send, 0))
    for bit in reversed(range(2, bits)):
        keep, send = add(keep, swap_bit(send, bit))

    order = [1, top, *range(2, top)]

    def near(keep, send):
        arrived = swap_bit(send, 1)
        gate_low = load(gate_weight, gate_weight.shape[0] * 4 // 7 // DEPTH * DEPTH, send)
        arrived, gate_low = lax.optimization_barrier((arrived, gate_low))
        normed, own = norm(here, keep, arrived, norm_gain)
        keep, send = feed(
            order, here, normed, swap_bit(normed, 0), own, gate_low, gate_weight, up_weight,
            down_weight,
        )
        keep, send = halve(keep, swap_bit(send, 0))
        keep, send = halve(keep, swap_bit(send, 1))
        return keep, swap_bit(send, top)

    def beside(movers):
        def branch(keep, send):
            if not movers:
                return *halve(*near(keep, send)), jnp.zeros_like(keys)
            keys_other = swap_bit(keys, top, lambda rank: movers >> rank % 4 & 1)
            some = keep[: keep.shape[0] // 4]
            keep, arrived = lax.cond(
                lengths[0] > 0, near, lambda *_: (some, some.astype(jnp.bfloat16)), keep, send
            )
            keep, send = halve(keep, arrived, LONG)
            keys_other, _ = lax.optimization_barrier((keys_other, send))
            return keep, send, keys_other

        return branch

    keep, send, keys_other = lax.switch(
        movers, [beside(movers) for movers in range(16)], keep, send
    )

    for bit in range(2, top - 1):
        keep, send = halve(keep, swap_bit(send, bit))
    layer_out = finish(keep, swap_bit(send, top - 1))
    held = hold(here, lengths, swap_flags, entry, keys, keys_other)
    return layer_out[None], jnp.swapaxes(held, 0, 1)[None]


def solution(mesh):
    placed = (
        P(("groups", "dp", "tp"), None, None),
        P("groups"),
        P(None, "groups"),
        P(None, ("groups", "dp", "tp"), None, None),
        P(None, ("groups", "dp", "tp"), None),
        P(None, ("groups", "dp", "tp"), None),
        P(),
        P(("dp", "tp"), None, None),
        P(("dp", "tp"), None),
        P(None, ("dp", "tp")),
        P(None, ("dp", "tp")),
        P(("dp", "tp"), None),
    )
    return jax.shard_map(
        local,
        mesh=mesh,
        in_specs=placed,
        out_specs=(P(None, ("groups", "dp", "tp"), None), P(("groups", "dp", "tp"), None, None)),
        check_vma=False,
    )
```

```python
import functools

import jax
import jax.numpy as jnp
from jax import lax
from jax.experimental import pallas as pl
from jax.experimental.pallas import tpu as pltpu
from jax.sharding import PartitionSpec as P

LATENT_WIDTH = 512
AXES = ("dp", "tp")
MIB = 1 << 20

VMEM = pl.BlockSpec(memory_space=pltpu.VMEM)
SMEM = pl.BlockSpec(memory_space=pltpu.SMEM)
ANY = pl.BlockSpec(memory_space=pl.ANY)
HBM = pl.BlockSpec(memory_space=pltpu.HBM)

FREE = pl.CostEstimate(flops=0, bytes_accessed=0, transcendentals=0)

LONG = pl.CostEstimate(flops=10**12, bytes_accessed=10**9, transcendentals=0)

score_scale = 0.07216878364870322


def in_vmem(array):
    return pltpu.with_memory_space_constraint(array, pltpu.VMEM)


def in_smem(array):
    return pltpu.with_memory_space_constraint(array, pltpu.SMEM)


def in_hbm(array):
    return pltpu.with_memory_space_constraint(array, pltpu.HBM)


def bytes_of(*arrays):
    return sum(array.size * array.dtype.itemsize for array in arrays)


def swap_bit(block, bit, take=lambda rank: True):
    ranks = lax.axis_size(AXES)
    route = [(rank, rank ^ 1 << bit) for rank in range(ranks) if take(rank)]
    return lax.ppermute(block, AXES, route)


def prepare_kernel(
    rank, lengths_hbm, flags_hbm, query_hbm, entry_hbm, keys_hbm,
    facts, movers, query, entry, keys, lengths, flags, sems,
):
    copies = [
        pltpu.make_async_copy(source, target, sems.at[index])
        for index, (source, target) in enumerate(
            [
                (lengths_hbm, lengths),
                (flags_hbm, flags),
                (query_hbm, query),
                (entry_hbm, entry),
                (keys_hbm, keys),
            ]
        )
    ]
    for copy in copies:
        copy.start()
    for copy in copies[:2]:
        copy.wait()
    slot = rank[0]
    facts[0] = lengths[slot]
    facts[1] = flags[0, slot]
    first = slot // 4 * 4
    movers[0] = sum(flags[0, first + each] * (1 << each) for each in range(4))
    for copy in copies[2:]:
        copy.wait()


def prepare(rank, lengths, flags, query, entry, keys):
    return pl.pallas_call(
        prepare_kernel,
        out_shape=(
            pltpu.SMEM((2,), jnp.int32),
            jax.ShapeDtypeStruct((1,), jnp.int32),
            pltpu.VMEM(query.shape, query.dtype),
            pltpu.VMEM(entry.shape, entry.dtype),
            pltpu.VMEM(keys.shape, keys.dtype),
        ),
        in_specs=[SMEM, HBM, HBM, HBM, HBM, HBM],
        out_specs=(SMEM, SMEM, VMEM, VMEM, VMEM),
        scratch_shapes=[
            pltpu.SMEM(lengths.shape, lengths.dtype),
            pltpu.SMEM(flags.shape, flags.dtype),
            pltpu.SemaphoreType.DMA((5,)),
        ],
        compiler_params=pltpu.CompilerParams(vmem_limit_bytes=MIB),
        cost_estimate=FREE,
        name="prepare",
    )(rank, in_hbm(lengths), in_hbm(flags), in_hbm(query), in_hbm(entry), in_hbm(keys))


def attend_kernel(facts, query, query_other, entry, entry_other, keys, context):
    live = facts[0]
    swapped = facts[1] == 1
    new_wide = jnp.where(
        swapped, entry_other[...].astype(jnp.float32), entry[...].astype(jnp.float32)
    )
    rows = jnp.where(swapped, query_other[...], query[...]).T
    new_score = jnp.sum(rows.astype(jnp.float32) * new_wide, axis=1, keepdims=True)
    keys_now = keys[...]
    scores = jnp.dot(rows, keys_now, preferred_element_type=jnp.float32)
    positions = lax.broadcasted_iota(jnp.int32, scores.shape, 1)
    scores = jnp.where(positions == live, new_score, scores) * score_scale
    scores = jnp.where(positions <= live, scores, -1e30)
    top = jnp.max(scores, axis=1, keepdims=True)
    weights = jnp.where(positions <= live, jnp.exp(scores - top), 0.0)
    total = jnp.sum(weights, axis=1, keepdims=True)
    probs = (weights / total).astype(jnp.bfloat16)
    new_prob = (jnp.exp(new_score * score_scale - top) / total).astype(jnp.bfloat16)
    probs = jnp.where(positions == live, jnp.zeros_like(probs), probs)
    result = lax.dot_general(
        probs,
        keys_now[:LATENT_WIDTH],
        (((1,), (1,)), ((), ())),
        preferred_element_type=jnp.float32,
    )
    result = result + new_prob.astype(jnp.float32) * new_wide[:, :LATENT_WIDTH]
    context[...] = result.astype(jnp.bfloat16)


def attend(facts, query, query_other, entry, entry_other, keys):
    heads = query.shape[1]
    return pl.pallas_call(
        attend_kernel,
        out_shape=jax.ShapeDtypeStruct((heads, LATENT_WIDTH), jnp.bfloat16),
        in_specs=[SMEM, VMEM, VMEM, VMEM, VMEM, VMEM],
        out_specs=VMEM,
        compiler_params=pltpu.CompilerParams(vmem_limit_bytes=12 * MIB),
        cost_estimate=FREE,
        name="attend",
    )(in_smem(facts), in_vmem(query), query_other, in_vmem(entry), entry_other, in_vmem(keys))


def project_kernel(
    rank, flags_hbm, per_head, expand_hbm, residual_hbm, weight,
    keep, send, flags, expand, residual, weight_here, values_here, sems, small_sems,
):
    heads, _, width = expand.shape
    rows = per_head.shape[0] // heads
    half = rows // 2
    small = [
        pltpu.make_async_copy(source, target, small_sems.at[index])
        for index, (source, target) in enumerate(
            [(flags_hbm, flags), (expand_hbm, expand), (residual_hbm, residual)]
        )
    ]
    parts = parts_of(weight.shape[1])
    copies = [
        pltpu.make_async_copy(weight.at[:, part], weight_here.at[:, part], sems.at[index])
        for index, part in enumerate(parts)
    ]
    for copy in small + copies:
        copy.start()
    for copy in small:
        copy.wait()
    bit = rank[0] % 2
    place = lax.broadcasted_iota(jnp.int32, (rows, 1), 0)
    source = jnp.zeros((rows, 1), jnp.int32)
    for position in range(rows):
        slot = 2 * position + bit if position < half else 2 * (position - half) + 1 - bit
        row = jnp.where(flags[0, slot] == 1, (slot + half) % rows, slot)
        source = jnp.where(place == position, row, source)
    lanes = lax.broadcasted_iota(jnp.int32, (rows, rows * heads), 1)
    pick = jnp.concatenate(
        [(lanes == source * heads + head).astype(jnp.float32) for head in range(heads)], axis=0
    ).astype(jnp.bfloat16)
    latent = jnp.dot(pick, per_head[...], preferred_element_type=jnp.float32).astype(jnp.bfloat16)
    for head in range(heads):
        values_here[:, head * width : (head + 1) * width] = jnp.dot(
            latent[head * rows : (head + 1) * rows],
            expand[head],
            preferred_element_type=jnp.float32,
        ).astype(jnp.bfloat16)
    mine = lax.broadcasted_iota(jnp.int32, (half, 1), 0) == rank[0] // 2

    for copy, part in zip(copies, parts):
        copy.wait()
        partial = jnp.dot(
            values_here[...], weight_here[:, part], preferred_element_type=jnp.float32
        )
        own = residual[:, part].astype(jnp.float32)
        keep[:, part] = partial[:half] + jnp.where(mine, own, 0.0)
        send[:, part] = partial[half:].astype(jnp.bfloat16)


def each_part(size, count, body):
    part = size // count

    @pl.loop(0, count)
    def _(index):
        body(index, pl.ds(pl.multiple_of(index * part, part), part))


def parts_of(size):
    cuts = [0, size // 2, size * 6 // 7, size]
    return [pl.ds(low, high - low) for low, high in zip(cuts, cuts[1:])]


def project(rank, flags, per_head, expand, weight, residual):
    rows, (depth, width) = per_head.shape[0] // expand.shape[0], weight.shape
    half = rows // 2
    return pl.pallas_call(
        project_kernel,
        out_shape=(
            jax.ShapeDtypeStruct((half, width), jnp.float32),
            jax.ShapeDtypeStruct((half, width), jnp.bfloat16),
        ),
        in_specs=[SMEM, HBM, VMEM, HBM, HBM, HBM],
        out_specs=(VMEM, VMEM),
        scratch_shapes=[
            pltpu.SMEM(flags.shape, flags.dtype),
            pltpu.VMEM(expand.shape, expand.dtype),
            pltpu.VMEM(residual.shape, residual.dtype),
            pltpu.VMEM(weight.shape, weight.dtype),
            pltpu.VMEM((rows, depth), jnp.bfloat16),
            pltpu.SemaphoreType.DMA((len(parts_of(width)),)),
            pltpu.SemaphoreType.DMA((3,)),
        ],
        compiler_params=pltpu.CompilerParams(vmem_limit_bytes=bytes_of(weight) + 10 * MIB),
        cost_estimate=FREE,
        name="project",
    )(
        rank, in_hbm(flags), per_head, in_hbm(expand), in_hbm(residual), in_hbm(weight)
    )


def add_kernel(keep, arrived, total, send):
    def body(index, here):
        result = keep[:, here] + arrived[:, here].astype(jnp.float32)
        total[:, here] = result
        send[:, here] = result.astype(send.dtype)

    each_part(keep.shape[1], 7, body)


def add(keep, arrived):
    return pl.pallas_call(
        add_kernel,
        out_shape=(
            jax.ShapeDtypeStruct(keep.shape, jnp.float32),
            jax.ShapeDtypeStruct(keep.shape, jnp.bfloat16),
        ),
        in_specs=[VMEM, VMEM],
        out_specs=(VMEM, VMEM),
        compiler_params=pltpu.CompilerParams(vmem_limit_bytes=8 * MIB),
        cost_estimate=FREE,
        name="add",
    )(keep, arrived)


def halve_kernel(keep, arrived, kept, send):
    half = keep.shape[0] // 2

    def body(index, here):
        total = keep[:, here] + arrived[:, here].astype(jnp.float32)
        kept[:, here] = total[:half]
        send[:, here] = total[half:].astype(send.dtype)

    each_part(keep.shape[1], 7, body)


def halve(keep, arrived, cost=FREE):
    shape = (keep.shape[0] // 2, keep.shape[1])
    return pl.pallas_call(
        halve_kernel,
        out_shape=(
            jax.ShapeDtypeStruct(shape, jnp.float32),
            jax.ShapeDtypeStruct(shape, jnp.bfloat16),
        ),
        in_specs=[VMEM, VMEM],
        out_specs=(VMEM, VMEM),
        compiler_params=pltpu.CompilerParams(vmem_limit_bytes=8 * MIB),
        cost_estimate=cost,
        name="halve",
    )(keep, arrived)


def finish_kernel(keep, arrived, out):
    out[...] = (keep[...] + arrived[...].astype(jnp.float32)).astype(out.dtype)


def finish(keep, arrived):
    return pl.pallas_call(
        finish_kernel,
        out_shape=jax.ShapeDtypeStruct(keep.shape, jnp.bfloat16),
        in_specs=[VMEM, VMEM],
        out_specs=VMEM,
        compiler_params=pltpu.CompilerParams(vmem_limit_bytes=8 * MIB),
        cost_estimate=FREE,
        name="finish",
    )(keep, arrived)


def load_kernel(first, source, after, target, sem):
    copy = pltpu.make_async_copy(source.at[pl.ds(first, target.shape[0])], target, sem)
    copy.start()
    copy.wait()


def load(array, first, rows, after):
    return pl.pallas_call(
        functools.partial(load_kernel, first),
        out_shape=pltpu.VMEM((rows, array.shape[1]), array.dtype),
        in_specs=[HBM, ANY],
        out_specs=VMEM,
        scratch_shapes=[pltpu.SemaphoreType.DMA],
        compiler_params=pltpu.CompilerParams(vmem_limit_bytes=MIB),
        cost_estimate=FREE,
        name="load_weight",
    )(in_hbm(array), after)


def norm_kernel(rank, keep, arrived, gain, normed, own, square):
    rows, width = keep.shape
    mine = lax.broadcasted_iota(jnp.int32, (rows, 1), 0) == rank[0] // 2
    square[...] = jnp.zeros_like(square)

    def measure(index, here):
        state = keep[:, here] + arrived[:, here].astype(jnp.float32)
        square[...] += jnp.sum(state * state, axis=1, keepdims=True)
        own[:, here] = jnp.sum(jnp.where(mine, state, 0.0), axis=0, keepdims=True)

    each_part(width, 7, measure)
    scale = lax.rsqrt(square[...] / width + 1e-06)

    def rescale(index, here):
        state = keep[:, here] + arrived[:, here].astype(jnp.float32)
        normed[:, here] = (state * scale * gain[:, here].astype(jnp.float32)).astype(normed.dtype)

    each_part(width, 7, rescale)


def norm(rank, keep, arrived, gain):
    return pl.pallas_call(
        norm_kernel,
        out_shape=(
            jax.ShapeDtypeStruct(keep.shape, jnp.bfloat16),
            jax.ShapeDtypeStruct((1, keep.shape[1]), jnp.float32),
        ),
        in_specs=[SMEM, VMEM, VMEM, VMEM],
        out_specs=(VMEM, VMEM),
        scratch_shapes=[pltpu.VMEM((keep.shape[0], 1), jnp.float32)],
        compiler_params=pltpu.CompilerParams(vmem_limit_bytes=8 * MIB),
        cost_estimate=FREE,
        name="norm",
    )(rank, keep, arrived, gain.reshape(1, -1))


DEPTH = 512
PARTS = 4


def feed_kernel(
    order, rank, mine, other, own, gate, up_low, up_high, down, keep, send, rows_here, down_here,
    hidden_here, sems,
):
    half = mine.shape[0]
    rows = 2 * half
    steps, low = gate.shape[0] // DEPTH, up_low.shape[0] // DEPTH
    width = down.shape[1]
    part = width // PARTS

    def depth(index):
        return pl.ds(pl.multiple_of(index * DEPTH, DEPTH), DEPTH)

    def down_copy(index, here):
        return pltpu.make_async_copy(down.at[:, here], down_here.at[:, here], sems.at[index])

    for index in range(PARTS):
        down_copy(index, pl.ds(index * part, part)).start()

    def place_rows(index, here):
        rows_here[:, here] = jnp.concatenate(
            [mine[:, here].astype(jnp.float32), other[:, here].astype(jnp.float32)], axis=0
        ).astype(jnp.bfloat16)

    each_part(mine.shape[1], 7, place_rows)

    def step(index, total, up_part):
        block = rows_here[:, depth(index)]
        return (
            total[0] + jnp.dot(block, gate[depth(index)], preferred_element_type=jnp.float32),
            total[1] + jnp.dot(block, up_part, preferred_element_type=jnp.float32),
        )

    def low_step(index, total):
        return step(index, total, up_low[depth(index)])

    def high_step(index, total):
        return step(index, total, up_high[depth(index - low)])

    zeros = jnp.zeros((rows, gate.shape[1]), jnp.float32)
    total = lax.fori_loop(0, low, low_step, (zeros, zeros))
    gated, upper = lax.fori_loop(low, steps, high_step, total)
    hidden = (gated * jax.nn.sigmoid(gated) * upper).astype(jnp.bfloat16)

    place = lax.broadcasted_iota(jnp.int32, (rows, 1), 0)
    source = jnp.zeros((rows, 1), jnp.int32)
    for position in range(rows):
        inner = position % half
        other_bits = sum(
            (inner >> len(order) - 1 - index & 1) << bit - 1 for index, bit in enumerate(order)
        )
        row = position - inner + ((rank[0] // 2) ^ other_bits)
        source = jnp.where(place == position, row, source)
    pick = (lax.broadcasted_iota(jnp.int32, (rows, rows), 1) == source).astype(jnp.bfloat16)
    hidden_here[...] = jnp.dot(pick, hidden, preferred_element_type=jnp.float32).astype(
        jnp.bfloat16
    )

    first = lax.broadcasted_iota(jnp.int32, (half, 1), 0) == 0

    def project_down(index, here):
        down_copy(index, here).wait()
        total = jnp.dot(hidden_here[...], down_here[:, here], preferred_element_type=jnp.float32)
        keep[:, here] = total[:half] + jnp.where(first, own[:, here], 0.0)
        send[:, here] = total[half:].astype(jnp.bfloat16)

    each_part(width, PARTS, project_down)


def feed(order, rank, mine, other, own, gate, up_low, up_high, down):
    half, width = mine.shape[0], down.shape[1]
    return pl.pallas_call(
        functools.partial(feed_kernel, order),
        out_shape=(
            jax.ShapeDtypeStruct((half, width), jnp.float32),
            jax.ShapeDtypeStruct((half, width), jnp.bfloat16),
        ),
        in_specs=[SMEM, VMEM, VMEM, VMEM, VMEM, VMEM, VMEM, HBM],
        out_specs=(VMEM, VMEM),
        scratch_shapes=[
            pltpu.VMEM((2 * half, mine.shape[1]), jnp.bfloat16),
            pltpu.VMEM(down.shape, down.dtype),
            pltpu.VMEM((2 * half, down.shape[0]), jnp.bfloat16),
            pltpu.SemaphoreType.DMA((PARTS,)),
        ],
        compiler_params=pltpu.CompilerParams(vmem_limit_bytes=bytes_of(down) + 6 * MIB),
        cost_estimate=FREE,
        name="feed",
    )(rank, mine, other, own, in_vmem(gate), in_vmem(up_low), in_vmem(up_high), in_hbm(down))


def hold_kernel(
    rank, lengths, flags, entry, own, arrived, held, block, fetched, stored
):
    slot = rank[0]
    ranks = lengths.shape[0]
    swapped = flags[0, slot] == 1
    position = lengths[jnp.where(swapped, (slot + ranks // 2) % ranks, slot)]

    parts = [pl.ds(low, own.shape[0] // 4) for low in range(0, own.shape[0], own.shape[0] // 4)]

    def fetch(source):
        for index, part in enumerate(parts):
            pltpu.make_async_copy(source.at[part], block.at[part], fetched.at[index]).start()

    @pl.when(swapped)
    def _():
        fetch(arrived)

    @pl.when(jnp.logical_not(swapped))
    def _():
        fetch(own)

    column = entry[...].astype(jnp.float32).T.astype(block.dtype)
    tile = position // 128
    here = pl.ds(pl.multiple_of(tile * 128, 128), 128)
    lanes = lax.broadcasted_iota(jnp.int32, (own.shape[0] // 4, 128), 1)
    stores = []
    for index, part in enumerate(parts):
        pltpu.make_async_copy(own.at[part], block.at[part], fetched.at[index]).wait()
        column_part = column[part.start : part.start + part.size]
        block[part, here] = jnp.where(lanes == position - tile * 128, column_part, block[part, here])
        store = pltpu.make_async_copy(block.at[part], held.at[part], stored.at[index])
        store.start()
        stores.append(store)
    for store in stores:
        store.wait()


def hold(rank, lengths, flags, entry, own, arrived):
    return pl.pallas_call(
        hold_kernel,
        out_shape=jax.ShapeDtypeStruct(own.shape, own.dtype),
        in_specs=[SMEM, SMEM, SMEM, VMEM, HBM, HBM],
        out_specs=ANY,
        scratch_shapes=[
            pltpu.VMEM(own.shape, own.dtype),
            pltpu.SemaphoreType.DMA((4,)),
            pltpu.SemaphoreType.DMA((4,)),
        ],
        compiler_params=pltpu.CompilerParams(vmem_limit_bytes=6 * MIB),
        cost_estimate=FREE,
        name="hold",
    )(rank, lengths, flags, entry, in_hbm(own), in_hbm(arrived))


def local(
    cache,
    lengths,
    swap_flags,
    queries,
    latents,
    residual,
    norm_gain,
    value_expand_weight,
    out_proj,
    gate_weight,
    up_weight,
    down_weight,
):
    ranks = lax.axis_size(AXES)
    bits = ranks.bit_length() - 1
    top = bits - 1
    rank = lax.axis_index(AXES)
    here = rank.reshape(1)
    keys = jnp.swapaxes(cache[0], 0, 1)
    query = jnp.swapaxes(queries[0, 0], 0, 1)
    entry = latents[0]

    query_other = swap_bit(query, top)
    entry_other = swap_bit(entry, top)
    facts, movers, *kept = prepare(here, lengths, swap_flags, query, entry, keys)
    query_other, facts, movers, *kept = lax.optimization_barrier(
        (query_other, facts, movers, *kept)
    )
    query_here, entry_here, keys_here = kept
    context = attend(facts, query_here, query_other, entry_here, entry_other, keys_here)

    heads = context.shape[0] // ranks
    per_head = lax.all_to_all(
        context.reshape(ranks, heads, LATENT_WIDTH), AXES, split_axis=0, concat_axis=0, tiled=True
    ).reshape(ranks * heads, LATENT_WIDTH)
    keep, send = project(here, swap_flags, per_head, value_expand_weight, out_proj, residual[0])

    keep, send = add(keep, swap_bit(send, 0))
    depth = up_weight.shape[0]
    low = depth * 4 // 7 // DEPTH * DEPTH
    for bit in reversed(range(2, bits)):
        arrived = swap_bit(send, bit)
        if bit == 2:
            up_low = load(up_weight, 0, low, send)
            arrived, up_low = lax.optimization_barrier((arrived, up_low))
        keep, send = add(keep, arrived)

    order = [1, top, *range(2, top)]

    def near(keep, send, up_low):
        arrived = swap_bit(send, 1)
        up_high = load(up_weight, low, depth - low, send)
        arrived, up_high = lax.optimization_barrier((arrived, up_high))
        normed, own = norm(here, keep, arrived, norm_gain)
        keep, send = feed(
            order, here, normed, swap_bit(normed, 0), own, gate_weight, up_low, up_high, down_weight
        )
        keep, send = halve(keep, swap_bit(send, 0))
        keep, send = halve(keep, swap_bit(send, 1))
        return keep, swap_bit(send, top)

    def beside(movers):
        def branch(keep, send, up_low):
            if not movers:
                return *halve(*near(keep, send, up_low)), jnp.zeros_like(keys)
            keys_other = swap_bit(keys, top, lambda rank: movers >> rank % 4 & 1)
            some = keep[: keep.shape[0] // 4]
            keep, arrived = lax.cond(
                lengths[0] > 0,
                near,
                lambda *_: (some, some.astype(jnp.bfloat16)),
                keep,
                send,
                up_low,
            )
            keep, send = halve(keep, arrived, LONG)
            keys_other, _ = lax.optimization_barrier((keys_other, send))
            return keep, send, keys_other

        return branch

    keep, send, keys_other = lax.switch(
        movers[0], [beside(movers) for movers in range(16)], keep, send, up_low
    )

    for bit in range(2, top - 1):
        keep, send = halve(keep, swap_bit(send, bit))
    layer_out = finish(keep, swap_bit(send, top - 1))
    held = hold(here, lengths, swap_flags, entry, keys, keys_other)
    return layer_out[None], jnp.swapaxes(held, 0, 1)[None]


def solution(mesh):
    placed = (
        P(("groups", "dp", "tp"), None, None),
        P("groups"),
        P(None, "groups"),
        P(None, ("groups", "dp", "tp"), None, None),
        P(None, ("groups", "dp", "tp"), None),
        P(None, ("groups", "dp", "tp"), None),
        P(),
        P(("dp", "tp"), None, None),
        P(("dp", "tp"), None),
        P(None, ("dp", "tp")),
        P(None, ("dp", "tp")),
        P(("dp", "tp"), None),
    )
    return jax.shard_map(
        local,
        mesh=mesh,
        in_specs=placed,
        out_specs=(P(None, ("groups", "dp", "tp"), None), P(("groups", "dp", "tp"), None, None)),
        check_vma=False,
    )
```

```python
import functools

import jax
import jax.numpy as jnp
from jax import lax
from jax.experimental import pallas as pl
from jax.experimental.pallas import tpu as pltpu
from jax.sharding import PartitionSpec as P

LATENT_WIDTH = 512
AXES = ("dp", "tp")
MIB = 1 << 20

VMEM = pl.BlockSpec(memory_space=pltpu.VMEM)
SMEM = pl.BlockSpec(memory_space=pltpu.SMEM)
ANY = pl.BlockSpec(memory_space=pl.ANY)
HBM = pl.BlockSpec(memory_space=pltpu.HBM)

FREE = pl.CostEstimate(flops=0, bytes_accessed=0, transcendentals=0)

LONG = pl.CostEstimate(flops=10**12, bytes_accessed=10**9, transcendentals=0)

score_scale = 0.07216878364870322


def in_vmem(array):
    return pltpu.with_memory_space_constraint(array, pltpu.VMEM)


def in_smem(array):
    return pltpu.with_memory_space_constraint(array, pltpu.SMEM)


def in_hbm(array):
    return pltpu.with_memory_space_constraint(array, pltpu.HBM)


def bytes_of(*arrays):
    return sum(array.size * array.dtype.itemsize for array in arrays)


def swap_bit(block, bit, take=lambda rank: True):
    ranks = lax.axis_size(AXES)
    route = [(rank, rank ^ 1 << bit) for rank in range(ranks) if take(rank)]
    return lax.ppermute(block, AXES, route)


def prepare_kernel(
    rank, lengths_hbm, flags_hbm, query_hbm, entry_hbm, keys_hbm,
    facts, movers, query, entry, keys, lengths, flags, sems,
):
    copies = [
        pltpu.make_async_copy(source, target, sems.at[index])
        for index, (source, target) in enumerate(
            [
                (lengths_hbm, lengths),
                (flags_hbm, flags),
                (query_hbm, query),
                (entry_hbm, entry),
                (keys_hbm, keys),
            ]
        )
    ]
    for copy in copies:
        copy.start()
    for copy in copies[:2]:
        copy.wait()
    slot = rank[0]
    facts[0] = lengths[slot]
    facts[1] = flags[0, slot]
    first = slot // 4 * 4
    movers[0] = sum(flags[0, first + each] * (1 << each) for each in range(4))
    for copy in copies[2:]:
        copy.wait()


def prepare(rank, lengths, flags, query, entry, keys):
    return pl.pallas_call(
        prepare_kernel,
        out_shape=(
            pltpu.SMEM((2,), jnp.int32),
            jax.ShapeDtypeStruct((1,), jnp.int32),
            pltpu.VMEM(query.shape, query.dtype),
            pltpu.VMEM(entry.shape, entry.dtype),
            pltpu.VMEM(keys.shape, keys.dtype),
        ),
        in_specs=[SMEM, HBM, HBM, HBM, HBM, HBM],
        out_specs=(SMEM, SMEM, VMEM, VMEM, VMEM),
        scratch_shapes=[
            pltpu.SMEM(lengths.shape, lengths.dtype),
            pltpu.SMEM(flags.shape, flags.dtype),
            pltpu.SemaphoreType.DMA((5,)),
        ],
        compiler_params=pltpu.CompilerParams(vmem_limit_bytes=MIB),
        cost_estimate=FREE,
        name="prepare",
    )(rank, in_hbm(lengths), in_hbm(flags), in_hbm(query), in_hbm(entry), in_hbm(keys))


def attend_kernel(facts, query, query_other, entry, entry_other, keys, context):
    live = facts[0]
    swapped = facts[1] == 1
    new_wide = jnp.where(
        swapped, entry_other[...].astype(jnp.float32), entry[...].astype(jnp.float32)
    )
    rows = jnp.where(swapped, query_other[...], query[...]).T
    new_score = jnp.sum(rows.astype(jnp.float32) * new_wide, axis=1, keepdims=True)
    keys_now = keys[...]
    scores = jnp.dot(rows, keys_now, preferred_element_type=jnp.float32)
    positions = lax.broadcasted_iota(jnp.int32, scores.shape, 1)
    scores = jnp.where(positions == live, new_score, scores) * score_scale
    scores = jnp.where(positions <= live, scores, -1e30)
    top = jnp.max(scores, axis=1, keepdims=True)
    weights = jnp.where(positions <= live, jnp.exp(scores - top), 0.0)
    total = jnp.sum(weights, axis=1, keepdims=True)
    probs = (weights / total).astype(jnp.bfloat16)
    new_prob = (jnp.exp(new_score * score_scale - top) / total).astype(jnp.bfloat16)
    probs = jnp.where(positions == live, jnp.zeros_like(probs), probs)
    result = lax.dot_general(
        probs,
        keys_now[:LATENT_WIDTH],
        (((1,), (1,)), ((), ())),
        preferred_element_type=jnp.float32,
    )
    result = result + new_prob.astype(jnp.float32) * new_wide[:, :LATENT_WIDTH]
    context[...] = result.astype(jnp.bfloat16)


def attend(facts, query, query_other, entry, entry_other, keys):
    heads = query.shape[1]
    return pl.pallas_call(
        attend_kernel,
        out_shape=jax.ShapeDtypeStruct((heads, LATENT_WIDTH), jnp.bfloat16),
        in_specs=[SMEM, VMEM, VMEM, VMEM, VMEM, VMEM],
        out_specs=VMEM,
        compiler_params=pltpu.CompilerParams(vmem_limit_bytes=12 * MIB),
        cost_estimate=FREE,
        name="attend",
    )(in_smem(facts), in_vmem(query), query_other, in_vmem(entry), entry_other, in_vmem(keys))


def project_kernel(
    rank, flags_hbm, per_head, expand_hbm, residual_hbm, weight,
    keep, send, flags, expand, residual, weight_here, values_here, sems, small_sems,
):
    heads, _, width = expand.shape
    rows = per_head.shape[0] // heads
    half = rows // 2
    small = [
        pltpu.make_async_copy(source, target, small_sems.at[index])
        for index, (source, target) in enumerate(
            [(flags_hbm, flags), (expand_hbm, expand), (residual_hbm, residual)]
        )
    ]
    parts = parts_of(weight.shape[1])
    copies = [
        pltpu.make_async_copy(weight.at[:, part], weight_here.at[:, part], sems.at[index])
        for index, part in enumerate(parts)
    ]
    for copy in small + copies:
        copy.start()
    for copy in small:
        copy.wait()
    bit = rank[0] % 2
    place = lax.broadcasted_iota(jnp.int32, (rows, 1), 0)
    source = jnp.zeros((rows, 1), jnp.int32)
    for position in range(rows):
        slot = 2 * position + bit if position < half else 2 * (position - half) + 1 - bit
        row = jnp.where(flags[0, slot] == 1, (slot + half) % rows, slot)
        source = jnp.where(place == position, row, source)
    lanes = lax.broadcasted_iota(jnp.int32, (rows, rows * heads), 1)
    pick = jnp.concatenate(
        [(lanes == source * heads + head).astype(jnp.float32) for head in range(heads)], axis=0
    ).astype(jnp.bfloat16)
    latent = jnp.dot(pick, per_head[...], preferred_element_type=jnp.float32).astype(jnp.bfloat16)
    for head in range(heads):
        values_here[:, head * width : (head + 1) * width] = jnp.dot(
            latent[head * rows : (head + 1) * rows],
            expand[head],
            preferred_element_type=jnp.float32,
        ).astype(jnp.bfloat16)
    mine = lax.broadcasted_iota(jnp.int32, (half, 1), 0) == rank[0] // 2

    for copy, part in zip(copies, parts):
        copy.wait()
        partial = jnp.dot(
            values_here[...], weight_here[:, part], preferred_element_type=jnp.float32
        )
        own = residual[:, part].astype(jnp.float32)
        keep[:, part] = partial[:half] + jnp.where(mine, own, 0.0)
        send[:, part] = partial[half:].astype(jnp.bfloat16)


def each_part(size, count, body):
    part = size // count

    @pl.loop(0, count)
    def _(index):
        body(index, pl.ds(pl.multiple_of(index * part, part), part))


def parts_of(size):
    cuts = [0, size * 4 // 7, size]
    return [pl.ds(low, high - low) for low, high in zip(cuts, cuts[1:])]


def project(rank, flags, per_head, expand, weight, residual):
    rows, (depth, width) = per_head.shape[0] // expand.shape[0], weight.shape
    half = rows // 2
    return pl.pallas_call(
        project_kernel,
        out_shape=(
            jax.ShapeDtypeStruct((half, width), jnp.float32),
            jax.ShapeDtypeStruct((half, width), jnp.bfloat16),
        ),
        in_specs=[SMEM, HBM, VMEM, HBM, HBM, HBM],
        out_specs=(VMEM, VMEM),
        scratch_shapes=[
            pltpu.SMEM(flags.shape, flags.dtype),
            pltpu.VMEM(expand.shape, expand.dtype),
            pltpu.VMEM(residual.shape, residual.dtype),
            pltpu.VMEM(weight.shape, weight.dtype),
            pltpu.VMEM((rows, depth), jnp.bfloat16),
            pltpu.SemaphoreType.DMA((len(parts_of(width)),)),
            pltpu.SemaphoreType.DMA((3,)),
        ],
        compiler_params=pltpu.CompilerParams(vmem_limit_bytes=bytes_of(weight) + 10 * MIB),
        cost_estimate=FREE,
        name="project",
    )(
        rank, in_hbm(flags), per_head, in_hbm(expand), in_hbm(residual), in_hbm(weight)
    )


def add_kernel(keep, arrived, total, send):
    def body(index, here):
        result = keep[:, here] + arrived[:, here].astype(jnp.float32)
        total[:, here] = result
        send[:, here] = result.astype(send.dtype)

    each_part(keep.shape[1], 7, body)


def add(keep, arrived):
    return pl.pallas_call(
        add_kernel,
        out_shape=(
            jax.ShapeDtypeStruct(keep.shape, jnp.float32),
            jax.ShapeDtypeStruct(keep.shape, jnp.bfloat16),
        ),
        in_specs=[VMEM, VMEM],
        out_specs=(VMEM, VMEM),
        compiler_params=pltpu.CompilerParams(vmem_limit_bytes=8 * MIB),
        cost_estimate=FREE,
        name="add",
    )(keep, arrived)


def halve_kernel(keep, arrived, kept, send):
    half = keep.shape[0] // 2

    def body(index, here):
        total = keep[:, here] + arrived[:, here].astype(jnp.float32)
        kept[:, here] = total[:half]
        send[:, here] = total[half:].astype(send.dtype)

    each_part(keep.shape[1], 7, body)


def halve(keep, arrived, cost=FREE):
    shape = (keep.shape[0] // 2, keep.shape[1])
    return pl.pallas_call(
        halve_kernel,
        out_shape=(
            jax.ShapeDtypeStruct(shape, jnp.float32),
            jax.ShapeDtypeStruct(shape, jnp.bfloat16),
        ),
        in_specs=[VMEM, VMEM],
        out_specs=(VMEM, VMEM),
        compiler_params=pltpu.CompilerParams(vmem_limit_bytes=8 * MIB),
        cost_estimate=cost,
        name="halve",
    )(keep, arrived)


def finish_kernel(keep, arrived, out):
    out[...] = (keep[...] + arrived[...].astype(jnp.float32)).astype(out.dtype)


def finish(keep, arrived):
    return pl.pallas_call(
        finish_kernel,
        out_shape=jax.ShapeDtypeStruct(keep.shape, jnp.bfloat16),
        in_specs=[VMEM, VMEM],
        out_specs=VMEM,
        compiler_params=pltpu.CompilerParams(vmem_limit_bytes=8 * MIB),
        cost_estimate=FREE,
        name="finish",
    )(keep, arrived)


def load_kernel(first, source, after, target, sem):
    copy = pltpu.make_async_copy(source.at[pl.ds(first, target.shape[0])], target, sem)
    copy.start()
    copy.wait()


def load(array, first, rows, after):
    return pl.pallas_call(
        functools.partial(load_kernel, first),
        out_shape=pltpu.VMEM((rows, array.shape[1]), array.dtype),
        in_specs=[HBM, ANY],
        out_specs=VMEM,
        scratch_shapes=[pltpu.SemaphoreType.DMA],
        compiler_params=pltpu.CompilerParams(vmem_limit_bytes=MIB),
        cost_estimate=FREE,
        name="load_weight",
    )(in_hbm(array), after)


def norm_kernel(rank, keep, arrived, gain, normed, own, square):
    rows, width = keep.shape
    mine = lax.broadcasted_iota(jnp.int32, (rows, 1), 0) == rank[0] // 2
    square[...] = jnp.zeros_like(square)

    def measure(index, here):
        state = keep[:, here] + arrived[:, here].astype(jnp.float32)
        square[...] += jnp.sum(state * state, axis=1, keepdims=True)
        own[:, here] = jnp.sum(jnp.where(mine, state, 0.0), axis=0, keepdims=True)

    each_part(width, 7, measure)
    scale = lax.rsqrt(square[...] / width + 1e-06)

    def rescale(index, here):
        state = keep[:, here] + arrived[:, here].astype(jnp.float32)
        normed[:, here] = (state * scale * gain[:, here].astype(jnp.float32)).astype(normed.dtype)

    each_part(width, 7, rescale)


def norm(rank, keep, arrived, gain):
    return pl.pallas_call(
        norm_kernel,
        out_shape=(
            jax.ShapeDtypeStruct(keep.shape, jnp.bfloat16),
            jax.ShapeDtypeStruct((1, keep.shape[1]), jnp.float32),
        ),
        in_specs=[SMEM, VMEM, VMEM, VMEM],
        out_specs=(VMEM, VMEM),
        scratch_shapes=[pltpu.VMEM((keep.shape[0], 1), jnp.float32)],
        compiler_params=pltpu.CompilerParams(vmem_limit_bytes=8 * MIB),
        cost_estimate=FREE,
        name="norm",
    )(rank, keep, arrived, gain.reshape(1, -1))


DEPTH = 512
PARTS = 4


def feed_kernel(
    order, rank, mine, other, own, gate, up_low, up_high, down, keep, send, rows_here, down_here,
    hidden_here, sems,
):
    half = mine.shape[0]
    rows = 2 * half
    steps, low = gate.shape[0] // DEPTH, up_low.shape[0] // DEPTH
    width = down.shape[1]
    part = width // PARTS

    def depth(index):
        return pl.ds(pl.multiple_of(index * DEPTH, DEPTH), DEPTH)

    def down_copy(index, here):
        return pltpu.make_async_copy(down.at[:, here], down_here.at[:, here], sems.at[index])

    for index in range(PARTS):
        down_copy(index, pl.ds(index * part, part)).start()

    def place_rows(index, here):
        rows_here[:, here] = jnp.concatenate(
            [mine[:, here].astype(jnp.float32), other[:, here].astype(jnp.float32)], axis=0
        ).astype(jnp.bfloat16)

    each_part(mine.shape[1], 7, place_rows)

    def step(index, total, up_part):
        block = rows_here[:, depth(index)]
        return (
            total[0] + jnp.dot(block, gate[depth(index)], preferred_element_type=jnp.float32),
            total[1] + jnp.dot(block, up_part, preferred_element_type=jnp.float32),
        )

    def low_step(index, total):
        return step(index, total, up_low[depth(index)])

    def high_step(index, total):
        return step(index, total, up_high[depth(index - low)])

    zeros = jnp.zeros((rows, gate.shape[1]), jnp.float32)
    total = lax.fori_loop(0, low, low_step, (zeros, zeros))
    gated, upper = lax.fori_loop(low, steps, high_step, total)
    hidden = (gated * jax.nn.sigmoid(gated) * upper).astype(jnp.bfloat16)

    place = lax.broadcasted_iota(jnp.int32, (rows, 1), 0)
    source = jnp.zeros((rows, 1), jnp.int32)
    for position in range(rows):
        inner = position % half
        other_bits = sum(
            (inner >> len(order) - 1 - index & 1) << bit - 1 for index, bit in enumerate(order)
        )
        row = position - inner + ((rank[0] // 2) ^ other_bits)
        source = jnp.where(place == position, row, source)
    pick = (lax.broadcasted_iota(jnp.int32, (rows, rows), 1) == source).astype(jnp.bfloat16)
    hidden_here[...] = jnp.dot(pick, hidden, preferred_element_type=jnp.float32).astype(
        jnp.bfloat16
    )

    first = lax.broadcasted_iota(jnp.int32, (half, 1), 0) == 0

    def project_down(index, here):
        down_copy(index, here).wait()
        total = jnp.dot(hidden_here[...], down_here[:, here], preferred_element_type=jnp.float32)
        keep[:, here] = total[:half] + jnp.where(first, own[:, here], 0.0)
        send[:, here] = total[half:].astype(jnp.bfloat16)

    each_part(width, PARTS, project_down)


def feed(order, rank, mine, other, own, gate, up_low, up_high, down):
    half, width = mine.shape[0], down.shape[1]
    return pl.pallas_call(
        functools.partial(feed_kernel, order),
        out_shape=(
            jax.ShapeDtypeStruct((half, width), jnp.float32),
            jax.ShapeDtypeStruct((half, width), jnp.bfloat16),
        ),
        in_specs=[SMEM, VMEM, VMEM, VMEM, VMEM, VMEM, VMEM, HBM],
        out_specs=(VMEM, VMEM),
        scratch_shapes=[
            pltpu.VMEM((2 * half, mine.shape[1]), jnp.bfloat16),
            pltpu.VMEM(down.shape, down.dtype),
            pltpu.VMEM((2 * half, down.shape[0]), jnp.bfloat16),
            pltpu.SemaphoreType.DMA((PARTS,)),
        ],
        compiler_params=pltpu.CompilerParams(vmem_limit_bytes=bytes_of(down) + 6 * MIB),
        cost_estimate=FREE,
        name="feed",
    )(rank, mine, other, own, in_vmem(gate), in_vmem(up_low), in_vmem(up_high), in_hbm(down))


def hold_kernel(
    rank, lengths, flags, entry, own, arrived, held, block, fetched, stored
):
    slot = rank[0]
    ranks = lengths.shape[0]
    swapped = flags[0, slot] == 1
    position = lengths[jnp.where(swapped, (slot + ranks // 2) % ranks, slot)]

    parts = [pl.ds(low, own.shape[0] // 4) for low in range(0, own.shape[0], own.shape[0] // 4)]

    def fetch(source):
        for index, part in enumerate(parts):
            pltpu.make_async_copy(source.at[part], block.at[part], fetched.at[index]).start()

    @pl.when(swapped)
    def _():
        fetch(arrived)

    @pl.when(jnp.logical_not(swapped))
    def _():
        fetch(own)

    column = entry[...].astype(jnp.float32).T.astype(block.dtype)
    tile = position // 128
    here = pl.ds(pl.multiple_of(tile * 128, 128), 128)
    lanes = lax.broadcasted_iota(jnp.int32, (own.shape[0] // 4, 128), 1)
    stores = []
    for index, part in enumerate(parts):
        pltpu.make_async_copy(own.at[part], block.at[part], fetched.at[index]).wait()
        column_part = column[part.start : part.start + part.size]
        block[part, here] = jnp.where(lanes == position - tile * 128, column_part, block[part, here])
        store = pltpu.make_async_copy(block.at[part], held.at[part], stored.at[index])
        store.start()
        stores.append(store)
    for store in stores:
        store.wait()


def hold(rank, lengths, flags, entry, own, arrived):
    return pl.pallas_call(
        hold_kernel,
        out_shape=jax.ShapeDtypeStruct(own.shape, own.dtype),
        in_specs=[SMEM, SMEM, SMEM, VMEM, HBM, HBM],
        out_specs=ANY,
        scratch_shapes=[
            pltpu.VMEM(own.shape, own.dtype),
            pltpu.SemaphoreType.DMA((4,)),
            pltpu.SemaphoreType.DMA((4,)),
        ],
        compiler_params=pltpu.CompilerParams(vmem_limit_bytes=6 * MIB),
        cost_estimate=FREE,
        name="hold",
    )(rank, lengths, flags, entry, in_hbm(own), in_hbm(arrived))


def local(
    cache,
    lengths,
    swap_flags,
    queries,
    latents,
    residual,
    norm_gain,
    value_expand_weight,
    out_proj,
    gate_weight,
    up_weight,
    down_weight,
):
    ranks = lax.axis_size(AXES)
    bits = ranks.bit_length() - 1
    top = bits - 1
    rank = lax.axis_index(AXES)
    here = rank.reshape(1)
    keys = jnp.swapaxes(cache[0], 0, 1)
    query = jnp.swapaxes(queries[0, 0], 0, 1)
    entry = latents[0]

    query_other = swap_bit(query, top)
    entry_other = swap_bit(entry, top)
    facts, movers, *kept = prepare(here, lengths, swap_flags, query, entry, keys)
    query_other, facts, movers, *kept = lax.optimization_barrier(
        (query_other, facts, movers, *kept)
    )
    query_here, entry_here, keys_here = kept
    context = attend(facts, query_here, query_other, entry_here, entry_other, keys_here)

    heads = context.shape[0] // ranks
    per_head = lax.all_to_all(
        context.reshape(ranks, heads, LATENT_WIDTH), AXES, split_axis=0, concat_axis=0, tiled=True
    ).reshape(ranks * heads, LATENT_WIDTH)
    keep, send = project(here, swap_flags, per_head, value_expand_weight, out_proj, residual[0])

    keep, send = add(keep, swap_bit(send, 0))
    depth = up_weight.shape[0]
    low = depth * 4 // 7 // DEPTH * DEPTH
    for bit in reversed(range(2, bits)):
        arrived = swap_bit(send, bit)
        if bit == 2:
            up_low = load(up_weight, 0, low, send)
            arrived, up_low = lax.optimization_barrier((arrived, up_low))
        keep, send = add(keep, arrived)

    order = [1, top, *range(2, top)]

    def near(keep, send, up_low):
        arrived = swap_bit(send, 1)
        up_high = load(up_weight, low, depth - low, send)
        arrived, up_high = lax.optimization_barrier((arrived, up_high))
        normed, own = norm(here, keep, arrived, norm_gain)
        keep, send = feed(
            order, here, normed, swap_bit(normed, 0), own, gate_weight, up_low, up_high, down_weight
        )
        keep, send = halve(keep, swap_bit(send, 0))
        keep, send = halve(keep, swap_bit(send, 1))
        return keep, swap_bit(send, top)

    def beside(movers):
        def branch(keep, send, up_low):
            if not movers:
                return *halve(*near(keep, send, up_low)), jnp.zeros_like(keys)
            keys_other = swap_bit(keys, top, lambda rank: movers >> rank % 4 & 1)
            some = keep[: keep.shape[0] // 4]
            keep, arrived = lax.cond(
                lengths[0] > 0,
                near,
                lambda *_: (some, some.astype(jnp.bfloat16)),
                keep,
                send,
                up_low,
            )
            keep, send = halve(keep, arrived, LONG)
            keys_other, _ = lax.optimization_barrier((keys_other, send))
            return keep, send, keys_other

        return branch

    keep, send, keys_other = lax.switch(
        movers[0], [beside(movers) for movers in range(16)], keep, send, up_low
    )

    for bit in range(2, top - 1):
        keep, send = halve(keep, swap_bit(send, bit))
    layer_out = finish(keep, swap_bit(send, top - 1))
    held = hold(here, lengths, swap_flags, entry, keys, keys_other)
    return layer_out[None], jnp.swapaxes(held, 0, 1)[None]


def solution(mesh):
    placed = (
        P(("groups", "dp", "tp"), None, None),
        P("groups"),
        P(None, "groups"),
        P(None, ("groups", "dp", "tp"), None, None),
        P(None, ("groups", "dp", "tp"), None),
        P(None, ("groups", "dp", "tp"), None),
        P(),
        P(("dp", "tp"), None, None),
        P(("dp", "tp"), None),
        P(None, ("dp", "tp")),
        P(None, ("dp", "tp")),
        P(("dp", "tp"), None),
    )
    return jax.shard_map(
        local,
        mesh=mesh,
        in_specs=placed,
        out_specs=(P(None, ("groups", "dp", "tp"), None), P(("groups", "dp", "tp"), None, None)),
        check_vma=False,
    )
```

```python
import functools

import jax
import jax.numpy as jnp
from jax import lax
from jax.experimental import pallas as pl
from jax.experimental.pallas import tpu as pltpu
from jax.sharding import PartitionSpec as P

LATENT_WIDTH = 512
AXES = ("dp", "tp")
MIB = 1 << 20

VMEM = pl.BlockSpec(memory_space=pltpu.VMEM)
SMEM = pl.BlockSpec(memory_space=pltpu.SMEM)
ANY = pl.BlockSpec(memory_space=pl.ANY)
HBM = pl.BlockSpec(memory_space=pltpu.HBM)

FREE = pl.CostEstimate(flops=0, bytes_accessed=0, transcendentals=0)

LONG = pl.CostEstimate(flops=10**12, bytes_accessed=10**9, transcendentals=0)

score_scale = 0.07216878364870322


def in_vmem(array):
    return pltpu.with_memory_space_constraint(array, pltpu.VMEM)


def in_smem(array):
    return pltpu.with_memory_space_constraint(array, pltpu.SMEM)


def in_hbm(array):
    return pltpu.with_memory_space_constraint(array, pltpu.HBM)


def bytes_of(*arrays):
    return sum(array.size * array.dtype.itemsize for array in arrays)


def swap_bit(block, bit, take=lambda rank: True):
    ranks = lax.axis_size(AXES)
    route = [(rank, rank ^ 1 << bit) for rank in range(ranks) if take(rank)]
    return lax.ppermute(block, AXES, route)


def prepare_kernel(
    rank, lengths_hbm, flags_hbm, query_hbm, entry_hbm, keys_hbm,
    facts, swapped, movers, query, entry, keys, early, late, lengths, flags, sems,
):
    copies = [
        pltpu.make_async_copy(source, target, sems.at[index])
        for index, (source, target) in enumerate(
            [
                (lengths_hbm, lengths),
                (flags_hbm, flags),
                (query_hbm, query),
                (entry_hbm, entry),
                (keys_hbm, keys),
            ]
        )
    ]
    for copy in copies:
        copy.start()
    for copy in copies[:2]:
        copy.wait()
    slot = rank[0]
    facts[0] = lengths[slot]
    facts[1] = flags[0, slot]
    swapped[0] = flags[0, slot]
    first = slot // 4 * 4
    movers[0] = sum(flags[0, first + each] * (1 << each) for each in range(4))
    for copy in copies[2:]:
        copy.wait()
    rows = early.shape[0]
    parts = [
        pltpu.make_async_copy(keys.at[pl.ds(0, rows)], early, sems.at[0]),
        pltpu.make_async_copy(keys.at[pl.ds(rows, late.shape[0])], late, sems.at[1]),
    ]
    for copy in parts:
        copy.start()
    for copy in parts:
        copy.wait()


EARLY = 96


def prepare(rank, lengths, flags, query, entry, keys):
    return pl.pallas_call(
        prepare_kernel,
        out_shape=(
            pltpu.SMEM((2,), jnp.int32),
            jax.ShapeDtypeStruct((1,), jnp.int32),
            jax.ShapeDtypeStruct((1,), jnp.int32),
            pltpu.VMEM(query.shape, query.dtype),
            pltpu.VMEM(entry.shape, entry.dtype),
            pltpu.VMEM(keys.shape, keys.dtype),
            pltpu.HBM((EARLY, keys.shape[1]), keys.dtype),
            pltpu.HBM((keys.shape[0] - EARLY, keys.shape[1]), keys.dtype),
        ),
        in_specs=[SMEM, HBM, HBM, HBM, HBM, HBM],
        out_specs=(SMEM, SMEM, SMEM, VMEM, VMEM, VMEM, HBM, HBM),
        scratch_shapes=[
            pltpu.SMEM(lengths.shape, lengths.dtype),
            pltpu.SMEM(flags.shape, flags.dtype),
            pltpu.SemaphoreType.DMA((5,)),
        ],
        compiler_params=pltpu.CompilerParams(vmem_limit_bytes=MIB),
        cost_estimate=FREE,
        name="prepare",
    )(rank, in_hbm(lengths), in_hbm(flags), in_hbm(query), in_hbm(entry), in_hbm(keys))


def attend_kernel(facts, query, query_other, entry, entry_other, keys, context):
    live = facts[0]
    swapped = facts[1] == 1
    new_wide = jnp.where(
        swapped, entry_other[...].astype(jnp.float32), entry[...].astype(jnp.float32)
    )
    rows = jnp.where(swapped, query_other[...], query[...]).T
    new_score = jnp.sum(rows.astype(jnp.float32) * new_wide, axis=1, keepdims=True)
    keys_now = keys[...]
    scores = jnp.dot(rows, keys_now, preferred_element_type=jnp.float32)
    positions = lax.broadcasted_iota(jnp.int32, scores.shape, 1)
    scores = jnp.where(positions == live, new_score, scores) * score_scale
    scores = jnp.where(positions <= live, scores, -1e30)
    top = jnp.max(scores, axis=1, keepdims=True)
    weights = jnp.where(positions <= live, jnp.exp(scores - top), 0.0)
    total = jnp.sum(weights, axis=1, keepdims=True)
    probs = (weights / total).astype(jnp.bfloat16)
    new_prob = (jnp.exp(new_score * score_scale - top) / total).astype(jnp.bfloat16)
    probs = jnp.where(positions == live, jnp.zeros_like(probs), probs)
    result = lax.dot_general(
        probs,
        keys_now[:LATENT_WIDTH],
        (((1,), (1,)), ((), ())),
        preferred_element_type=jnp.float32,
    )
    result = result + new_prob.astype(jnp.float32) * new_wide[:, :LATENT_WIDTH]
    context[...] = result.astype(jnp.bfloat16)


def attend(facts, query, query_other, entry, entry_other, keys):
    heads = query.shape[1]
    return pl.pallas_call(
        attend_kernel,
        out_shape=jax.ShapeDtypeStruct((heads, LATENT_WIDTH), jnp.bfloat16),
        in_specs=[SMEM, VMEM, VMEM, VMEM, VMEM, VMEM],
        out_specs=VMEM,
        compiler_params=pltpu.CompilerParams(vmem_limit_bytes=12 * MIB),
        cost_estimate=FREE,
        name="attend",
    )(in_smem(facts), in_vmem(query), query_other, in_vmem(entry), entry_other, in_vmem(keys))


def project_kernel(
    rank, flags_hbm, per_head, expand_hbm, residual_hbm, weight,
    keep, send, flags, expand, residual, weight_here, values_here, sems, small_sems,
):
    heads, _, width = expand.shape
    rows = per_head.shape[0] // heads
    half = rows // 2
    small = [
        pltpu.make_async_copy(source, target, small_sems.at[index])
        for index, (source, target) in enumerate(
            [(flags_hbm, flags), (expand_hbm, expand), (residual_hbm, residual)]
        )
    ]
    parts = parts_of(weight.shape[1])
    copies = [
        pltpu.make_async_copy(weight.at[:, part], weight_here.at[:, part], sems.at[index])
        for index, part in enumerate(parts)
    ]
    for copy in small + copies:
        copy.start()
    for copy in small:
        copy.wait()
    bit = rank[0] % 2
    place = lax.broadcasted_iota(jnp.int32, (rows, 1), 0)
    source = jnp.zeros((rows, 1), jnp.int32)
    for position in range(rows):
        slot = 2 * position + bit if position < half else 2 * (position - half) + 1 - bit
        row = jnp.where(flags[0, slot] == 1, (slot + half) % rows, slot)
        source = jnp.where(place == position, row, source)
    lanes = lax.broadcasted_iota(jnp.int32, (rows, rows * heads), 1)
    pick = jnp.concatenate(
        [(lanes == source * heads + head).astype(jnp.float32) for head in range(heads)], axis=0
    ).astype(jnp.bfloat16)
    latent = jnp.dot(pick, per_head[...], preferred_element_type=jnp.float32).astype(jnp.bfloat16)
    for head in range(heads):
        values_here[:, head * width : (head + 1) * width] = jnp.dot(
            latent[head * rows : (head + 1) * rows],
            expand[head],
            preferred_element_type=jnp.float32,
        ).astype(jnp.bfloat16)
    mine = lax.broadcasted_iota(jnp.int32, (half, 1), 0) == rank[0] // 2

    for copy, part in zip(copies, parts):
        copy.wait()
        partial = jnp.dot(
            values_here[...], weight_here[:, part], preferred_element_type=jnp.float32
        )
        own = residual[:, part].astype(jnp.float32)
        keep[:, part] = partial[:half] + jnp.where(mine, own, 0.0)
        send[:, part] = partial[half:].astype(jnp.bfloat16)


def each_part(size, count, body):
    part = size // count

    @pl.loop(0, count)
    def _(index):
        body(index, pl.ds(pl.multiple_of(index * part, part), part))


def parts_of(size):
    cuts = [0, size * 4 // 7, size]
    return [pl.ds(low, high - low) for low, high in zip(cuts, cuts[1:])]


def project(rank, flags, per_head, expand, weight, residual):
    rows, (depth, width) = per_head.shape[0] // expand.shape[0], weight.shape
    half = rows // 2
    return pl.pallas_call(
        project_kernel,
        out_shape=(
            jax.ShapeDtypeStruct((half, width), jnp.float32),
            jax.ShapeDtypeStruct((half, width), jnp.bfloat16),
        ),
        in_specs=[SMEM, HBM, VMEM, HBM, HBM, HBM],
        out_specs=(VMEM, VMEM),
        scratch_shapes=[
            pltpu.SMEM(flags.shape, flags.dtype),
            pltpu.VMEM(expand.shape, expand.dtype),
            pltpu.VMEM(residual.shape, residual.dtype),
            pltpu.VMEM(weight.shape, weight.dtype),
            pltpu.VMEM((rows, depth), jnp.bfloat16),
            pltpu.SemaphoreType.DMA((len(parts_of(width)),)),
            pltpu.SemaphoreType.DMA((3,)),
        ],
        compiler_params=pltpu.CompilerParams(vmem_limit_bytes=bytes_of(weight) + 10 * MIB),
        cost_estimate=FREE,
        name="project",
    )(
        rank, in_hbm(flags), per_head, in_hbm(expand), in_hbm(residual), in_hbm(weight)
    )


def add_kernel(keep, arrived, total, send):
    def body(index, here):
        result = keep[:, here] + arrived[:, here].astype(jnp.float32)
        total[:, here] = result
        send[:, here] = result.astype(send.dtype)

    each_part(keep.shape[1], 7, body)


def add(keep, arrived):
    return pl.pallas_call(
        add_kernel,
        out_shape=(
            jax.ShapeDtypeStruct(keep.shape, jnp.float32),
            jax.ShapeDtypeStruct(keep.shape, jnp.bfloat16),
        ),
        in_specs=[VMEM, VMEM],
        out_specs=(VMEM, VMEM),
        compiler_params=pltpu.CompilerParams(vmem_limit_bytes=8 * MIB),
        cost_estimate=FREE,
        name="add",
    )(keep, arrived)


def halve_kernel(keep, arrived, kept, send):
    half = keep.shape[0] // 2

    def body(index, here):
        total = keep[:, here] + arrived[:, here].astype(jnp.float32)
        kept[:, here] = total[:half]
        send[:, here] = total[half:].astype(send.dtype)

    each_part(keep.shape[1], 7, body)


def halve(keep, arrived, cost=FREE):
    shape = (keep.shape[0] // 2, keep.shape[1])
    return pl.pallas_call(
        halve_kernel,
        out_shape=(
            jax.ShapeDtypeStruct(shape, jnp.float32),
            jax.ShapeDtypeStruct(shape, jnp.bfloat16),
        ),
        in_specs=[VMEM, VMEM],
        out_specs=(VMEM, VMEM),
        compiler_params=pltpu.CompilerParams(vmem_limit_bytes=8 * MIB),
        cost_estimate=cost,
        name="halve",
    )(keep, arrived)


def finish_kernel(keep, arrived, out):
    out[...] = (keep[...] + arrived[...].astype(jnp.float32)).astype(out.dtype)


def finish(keep, arrived):
    return pl.pallas_call(
        finish_kernel,
        out_shape=jax.ShapeDtypeStruct(keep.shape, jnp.bfloat16),
        in_specs=[VMEM, VMEM],
        out_specs=VMEM,
        compiler_params=pltpu.CompilerParams(vmem_limit_bytes=8 * MIB),
        cost_estimate=FREE,
        name="finish",
    )(keep, arrived)


def load_kernel(first, source, after, target, sem):
    copy = pltpu.make_async_copy(source.at[pl.ds(first, target.shape[0])], target, sem)
    copy.start()
    copy.wait()


def load(array, first, rows, after):
    return pl.pallas_call(
        functools.partial(load_kernel, first),
        out_shape=pltpu.VMEM((rows, array.shape[1]), array.dtype),
        in_specs=[HBM, ANY],
        out_specs=VMEM,
        scratch_shapes=[pltpu.SemaphoreType.DMA],
        compiler_params=pltpu.CompilerParams(vmem_limit_bytes=MIB),
        cost_estimate=FREE,
        name="load_weight",
    )(in_hbm(array), after)


def norm_kernel(rank, keep, arrived, gain, normed, own, square):
    rows, width = keep.shape
    mine = lax.broadcasted_iota(jnp.int32, (rows, 1), 0) == rank[0] // 2
    square[...] = jnp.zeros_like(square)

    def measure(index, here):
        state = keep[:, here] + arrived[:, here].astype(jnp.float32)
        square[...] += jnp.sum(state * state, axis=1, keepdims=True)
        own[:, here] = jnp.sum(jnp.where(mine, state, 0.0), axis=0, keepdims=True)

    each_part(width, 7, measure)
    scale = lax.rsqrt(square[...] / width + 1e-06)

    def rescale(index, here):
        state = keep[:, here] + arrived[:, here].astype(jnp.float32)
        normed[:, here] = (state * scale * gain[:, here].astype(jnp.float32)).astype(normed.dtype)

    each_part(width, 7, rescale)


def norm(rank, keep, arrived, gain):
    return pl.pallas_call(
        norm_kernel,
        out_shape=(
            jax.ShapeDtypeStruct(keep.shape, jnp.bfloat16),
            jax.ShapeDtypeStruct((1, keep.shape[1]), jnp.float32),
        ),
        in_specs=[SMEM, VMEM, VMEM, VMEM],
        out_specs=(VMEM, VMEM),
        scratch_shapes=[pltpu.VMEM((keep.shape[0], 1), jnp.float32)],
        compiler_params=pltpu.CompilerParams(vmem_limit_bytes=8 * MIB),
        cost_estimate=FREE,
        name="norm",
    )(rank, keep, arrived, gain.reshape(1, -1))


DEPTH = 512
PARTS = 4


def feed_kernel(
    order, rank, mine, other, own, gate, up_low, up_high, down, keep, send, rows_here, down_here,
    hidden_here, sems,
):
    half = mine.shape[0]
    rows = 2 * half
    steps, low = gate.shape[0] // DEPTH, up_low.shape[0] // DEPTH
    width = down.shape[1]
    part = width // PARTS

    def depth(index):
        return pl.ds(pl.multiple_of(index * DEPTH, DEPTH), DEPTH)

    def down_copy(index, here):
        return pltpu.make_async_copy(down.at[:, here], down_here.at[:, here], sems.at[index])

    for index in range(PARTS):
        down_copy(index, pl.ds(index * part, part)).start()

    def place_rows(index, here):
        rows_here[:, here] = jnp.concatenate(
            [mine[:, here].astype(jnp.float32), other[:, here].astype(jnp.float32)], axis=0
        ).astype(jnp.bfloat16)

    each_part(mine.shape[1], 7, place_rows)

    def step(index, total, up_part):
        block = rows_here[:, depth(index)]
        return (
            total[0] + jnp.dot(block, gate[depth(index)], preferred_element_type=jnp.float32),
            total[1] + jnp.dot(block, up_part, preferred_element_type=jnp.float32),
        )

    def low_step(index, total):
        return step(index, total, up_low[depth(index)])

    def high_step(index, total):
        return step(index, total, up_high[depth(index - low)])

    zeros = jnp.zeros((rows, gate.shape[1]), jnp.float32)
    total = lax.fori_loop(0, low, low_step, (zeros, zeros))
    gated, upper = lax.fori_loop(low, steps, high_step, total)
    hidden = (gated * jax.nn.sigmoid(gated) * upper).astype(jnp.bfloat16)

    place = lax.broadcasted_iota(jnp.int32, (rows, 1), 0)
    source = jnp.zeros((rows, 1), jnp.int32)
    for position in range(rows):
        inner = position % half
        other_bits = sum(
            (inner >> len(order) - 1 - index & 1) << bit - 1 for index, bit in enumerate(order)
        )
        row = position - inner + ((rank[0] // 2) ^ other_bits)
        source = jnp.where(place == position, row, source)
    pick = (lax.broadcasted_iota(jnp.int32, (rows, rows), 1) == source).astype(jnp.bfloat16)
    hidden_here[...] = jnp.dot(pick, hidden, preferred_element_type=jnp.float32).astype(
        jnp.bfloat16
    )

    first = lax.broadcasted_iota(jnp.int32, (half, 1), 0) == 0

    def project_down(index, here):
        down_copy(index, here).wait()
        total = jnp.dot(hidden_here[...], down_here[:, here], preferred_element_type=jnp.float32)
        keep[:, here] = total[:half] + jnp.where(first, own[:, here], 0.0)
        send[:, here] = total[half:].astype(jnp.bfloat16)

    each_part(width, PARTS, project_down)


def feed(order, rank, mine, other, own, gate, up_low, up_high, down):
    half, width = mine.shape[0], down.shape[1]
    return pl.pallas_call(
        functools.partial(feed_kernel, order),
        out_shape=(
            jax.ShapeDtypeStruct((half, width), jnp.float32),
            jax.ShapeDtypeStruct((half, width), jnp.bfloat16),
        ),
        in_specs=[SMEM, VMEM, VMEM, VMEM, VMEM, VMEM, VMEM, HBM],
        out_specs=(VMEM, VMEM),
        scratch_shapes=[
            pltpu.VMEM((2 * half, mine.shape[1]), jnp.bfloat16),
            pltpu.VMEM(down.shape, down.dtype),
            pltpu.VMEM((2 * half, down.shape[0]), jnp.bfloat16),
            pltpu.SemaphoreType.DMA((PARTS,)),
        ],
        compiler_params=pltpu.CompilerParams(vmem_limit_bytes=bytes_of(down) + 6 * MIB),
        cost_estimate=FREE,
        name="feed",
    )(rank, mine, other, own, in_vmem(gate), in_vmem(up_low), in_vmem(up_high), in_hbm(down))


def hold_kernel(
    rank, lengths, flags, entry, own, early, late, held, block, fetched, stored
):
    slot = rank[0]
    ranks = lengths.shape[0]
    swapped = flags[0, slot] == 1
    position = lengths[jnp.where(swapped, (slot + ranks // 2) % ranks, slot)]

    cut = early.shape[0]
    size = late.shape[0] // 3
    parts = [pl.ds(0, cut), *(pl.ds(cut + size * index, size) for index in range(3))]

    @pl.when(swapped)
    def _():
        pltpu.make_async_copy(early, block.at[parts[0]], fetched.at[0]).start()
        for index, part in enumerate(parts[1:]):
            source = late.at[pl.ds(size * index, size)]
            pltpu.make_async_copy(source, block.at[part], fetched.at[index + 1]).start()

    @pl.when(jnp.logical_not(swapped))
    def _():
        for index, part in enumerate(parts):
            pltpu.make_async_copy(own.at[part], block.at[part], fetched.at[index]).start()

    column = entry[...].astype(jnp.float32).T.astype(block.dtype)
    tile = position // 128
    here = pl.ds(pl.multiple_of(tile * 128, 128), 128)
    stores = []
    for index, part in enumerate(parts):
        pltpu.make_async_copy(own.at[part], block.at[part], fetched.at[index]).wait()
        column_part = column[part.start : part.start + part.size]
        lanes = lax.broadcasted_iota(jnp.int32, (part.size, 128), 1)
        block[part, here] = jnp.where(lanes == position - tile * 128, column_part, block[part, here])
        store = pltpu.make_async_copy(block.at[part], held.at[part], stored.at[index])
        store.start()
        stores.append(store)
    for store in stores:
        store.wait()


def hold(rank, lengths, flags, entry, own, early, late):
    return pl.pallas_call(
        hold_kernel,
        out_shape=jax.ShapeDtypeStruct(own.shape, own.dtype),
        in_specs=[SMEM, SMEM, SMEM, VMEM, HBM, HBM, HBM],
        out_specs=ANY,
        scratch_shapes=[
            pltpu.VMEM(own.shape, own.dtype),
            pltpu.SemaphoreType.DMA((5,)),
            pltpu.SemaphoreType.DMA((5,)),
        ],
        compiler_params=pltpu.CompilerParams(vmem_limit_bytes=6 * MIB),
        cost_estimate=FREE,
        name="hold",
    )(rank, lengths, flags, entry, in_hbm(own), in_hbm(early), in_hbm(late))


def local(
    cache,
    lengths,
    swap_flags,
    queries,
    latents,
    residual,
    norm_gain,
    value_expand_weight,
    out_proj,
    gate_weight,
    up_weight,
    down_weight,
):
    ranks = lax.axis_size(AXES)
    bits = ranks.bit_length() - 1
    top = bits - 1
    rank = lax.axis_index(AXES)
    here = rank.reshape(1)
    keys = jnp.swapaxes(cache[0], 0, 1)
    query = jnp.swapaxes(queries[0, 0], 0, 1)
    entry = latents[0]

    query_other = swap_bit(query, top)
    entry_other = swap_bit(entry, top)
    facts, swapped, movers, *kept, early, late = prepare(
        here, lengths, swap_flags, query, entry, keys
    )
    query_other, facts, swapped, movers, *kept = lax.optimization_barrier(
        (query_other, facts, swapped, movers, *kept)
    )
    query_here, entry_here, keys_here = kept
    context = attend(facts, query_here, query_other, entry_here, entry_other, keys_here)

    heads = context.shape[0] // ranks
    per_head = lax.all_to_all(
        context.reshape(ranks, heads, LATENT_WIDTH), AXES, split_axis=0, concat_axis=0, tiled=True
    ).reshape(ranks * heads, LATENT_WIDTH)
    def projected(per_head):
        return project(here, swap_flags, per_head, value_expand_weight, out_proj, residual[0])

    def moving(per_head):
        early_other = swap_bit(early, top)
        return *projected(per_head), early_other

    def staying(per_head):
        return *projected(per_head), jnp.zeros_like(early)

    keep, send, early_other = lax.cond(swapped[0] == 1, moving, staying, per_head)

    keep, send = add(keep, swap_bit(send, 0))
    depth = up_weight.shape[0]
    low = depth * 4 // 7 // DEPTH * DEPTH
    for bit in reversed(range(2, bits)):
        arrived = swap_bit(send, bit)
        if bit == top:
            up_low = load(up_weight, 0, low, send)
            arrived, up_low = lax.optimization_barrier((arrived, up_low))
        keep, send = add(keep, arrived)

    order = [1, top, *range(2, top)]

    def near(keep, send, up_low):
        arrived = swap_bit(send, 1)
        up_high = load(up_weight, low, depth - low, send)
        arrived, up_high = lax.optimization_barrier((arrived, up_high))
        normed, own = norm(here, keep, arrived, norm_gain)
        keep, send = feed(
            order, here, normed, swap_bit(normed, 0), own, gate_weight, up_low, up_high, down_weight
        )
        keep, send = halve(keep, swap_bit(send, 0))
        keep, send = halve(keep, swap_bit(send, 1))
        return keep, swap_bit(send, top)

    def beside(movers):
        def branch(keep, send, up_low):
            if not movers:
                return *halve(*near(keep, send, up_low)), jnp.zeros_like(late)
            late_other = swap_bit(late, top, lambda rank: movers >> rank % 4 & 1)
            some = keep[: keep.shape[0] // 4]
            keep, arrived = lax.cond(
                lengths[0] > 0,
                near,
                lambda *_: (some, some.astype(jnp.bfloat16)),
                keep,
                send,
                up_low,
            )
            keep, send = halve(keep, arrived, LONG)
            late_other, _ = lax.optimization_barrier((late_other, send))
            return keep, send, late_other

        return branch

    keep, send, late_other = lax.switch(
        movers[0], [beside(movers) for movers in range(16)], keep, send, up_low
    )

    for bit in range(2, top - 1):
        keep, send = halve(keep, swap_bit(send, bit))
    layer_out = finish(keep, swap_bit(send, top - 1))
    held = hold(here, lengths, swap_flags, entry, keys, early_other, late_other)
    return layer_out[None], jnp.swapaxes(held, 0, 1)[None]


def solution(mesh):
    placed = (
        P(("groups", "dp", "tp"), None, None),
        P("groups"),
        P(None, "groups"),
        P(None, ("groups", "dp", "tp"), None, None),
        P(None, ("groups", "dp", "tp"), None),
        P(None, ("groups", "dp", "tp"), None),
        P(),
        P(("dp", "tp"), None, None),
        P(("dp", "tp"), None),
        P(None, ("dp", "tp")),
        P(None, ("dp", "tp")),
        P(("dp", "tp"), None),
    )
    return jax.shard_map(
        local,
        mesh=mesh,
        in_specs=placed,
        out_specs=(P(None, ("groups", "dp", "tp"), None), P(("groups", "dp", "tp"), None, None)),
        check_vma=False,
    )
```

```python
import functools

import jax
import jax.numpy as jnp
from jax import lax
from jax.experimental import pallas as pl
from jax.experimental.pallas import tpu as pltpu
from jax.sharding import PartitionSpec as P

LATENT_WIDTH = 512
AXES = ("dp", "tp")
MIB = 1 << 20

VMEM = pl.BlockSpec(memory_space=pltpu.VMEM)
SMEM = pl.BlockSpec(memory_space=pltpu.SMEM)
ANY = pl.BlockSpec(memory_space=pl.ANY)
HBM = pl.BlockSpec(memory_space=pltpu.HBM)

FREE = pl.CostEstimate(flops=0, bytes_accessed=0, transcendentals=0)

LONG = pl.CostEstimate(flops=10**12, bytes_accessed=10**9, transcendentals=0)

score_scale = 0.07216878364870322


def in_vmem(array):
    return pltpu.with_memory_space_constraint(array, pltpu.VMEM)


def in_smem(array):
    return pltpu.with_memory_space_constraint(array, pltpu.SMEM)


def in_hbm(array):
    return pltpu.with_memory_space_constraint(array, pltpu.HBM)


def bytes_of(*arrays):
    return sum(array.size * array.dtype.itemsize for array in arrays)


def swap_bit(block, bit, take=lambda rank: True):
    ranks = lax.axis_size(AXES)
    route = [(rank, rank ^ 1 << bit) for rank in range(ranks) if take(rank)]
    return lax.ppermute(block, AXES, route)


def prepare_kernel(
    rank, lengths_hbm, flags_hbm, query_hbm, entry_hbm, keys_hbm,
    facts, swapped, movers, query, entry, keys, early, late, lengths, flags, sems,
):
    copies = [
        pltpu.make_async_copy(source, target, sems.at[index])
        for index, (source, target) in enumerate(
            [
                (lengths_hbm, lengths),
                (flags_hbm, flags),
                (query_hbm, query),
                (entry_hbm, entry),
                (keys_hbm, keys),
            ]
        )
    ]
    for copy in copies:
        copy.start()
    for copy in copies[:2]:
        copy.wait()
    slot = rank[0]
    facts[0] = lengths[slot]
    facts[1] = flags[0, slot]
    swapped[0] = flags[0, slot]
    first = slot // 4 * 4
    movers[0] = sum(flags[0, first + each] * (1 << each) for each in range(4))
    for copy in copies[2:]:
        copy.wait()
    rows = early.shape[0]
    parts = [
        pltpu.make_async_copy(keys.at[pl.ds(0, rows)], early, sems.at[0]),
        pltpu.make_async_copy(keys.at[pl.ds(rows, late.shape[0])], late, sems.at[1]),
    ]
    for copy in parts:
        copy.start()
    for copy in parts:
        copy.wait()


EARLY = 96


def prepare(rank, lengths, flags, query, entry, keys):
    return pl.pallas_call(
        prepare_kernel,
        out_shape=(
            pltpu.SMEM((2,), jnp.int32),
            jax.ShapeDtypeStruct((1,), jnp.int32),
            jax.ShapeDtypeStruct((1,), jnp.int32),
            pltpu.VMEM(query.shape, query.dtype),
            pltpu.VMEM(entry.shape, entry.dtype),
            pltpu.VMEM(keys.shape, keys.dtype),
            pltpu.HBM((EARLY, keys.shape[1]), keys.dtype),
            pltpu.HBM((keys.shape[0] - EARLY, keys.shape[1]), keys.dtype),
        ),
        in_specs=[SMEM, HBM, HBM, HBM, HBM, HBM],
        out_specs=(SMEM, SMEM, SMEM, VMEM, VMEM, VMEM, HBM, HBM),
        scratch_shapes=[
            pltpu.SMEM(lengths.shape, lengths.dtype),
            pltpu.SMEM(flags.shape, flags.dtype),
            pltpu.SemaphoreType.DMA((5,)),
        ],
        compiler_params=pltpu.CompilerParams(vmem_limit_bytes=MIB),
        cost_estimate=FREE,
        name="prepare",
    )(rank, in_hbm(lengths), in_hbm(flags), in_hbm(query), in_hbm(entry), in_hbm(keys))


def attend_kernel(facts, query, query_other, entry, entry_other, keys, context):
    live = facts[0]
    swapped = facts[1] == 1
    new_wide = jnp.where(
        swapped, entry_other[...].astype(jnp.float32), entry[...].astype(jnp.float32)
    )
    rows = jnp.where(swapped, query_other[...], query[...]).T
    new_score = jnp.sum(rows.astype(jnp.float32) * new_wide, axis=1, keepdims=True)
    keys_now = keys[...]
    scores = jnp.dot(rows, keys_now, preferred_element_type=jnp.float32)
    positions = lax.broadcasted_iota(jnp.int32, scores.shape, 1)
    scores = jnp.where(positions == live, new_score, scores) * score_scale
    scores = jnp.where(positions <= live, scores, -1e30)
    top = jnp.max(scores, axis=1, keepdims=True)
    weights = jnp.where(positions <= live, jnp.exp(scores - top), 0.0)
    total = jnp.sum(weights, axis=1, keepdims=True)
    probs = (weights / total).astype(jnp.bfloat16)
    new_prob = (jnp.exp(new_score * score_scale - top) / total).astype(jnp.bfloat16)
    probs = jnp.where(positions == live, jnp.zeros_like(probs), probs)
    result = lax.dot_general(
        probs,
        keys_now[:LATENT_WIDTH],
        (((1,), (1,)), ((), ())),
        preferred_element_type=jnp.float32,
    )
    result = result + new_prob.astype(jnp.float32) * new_wide[:, :LATENT_WIDTH]
    context[...] = result.astype(jnp.bfloat16)


def attend(facts, query, query_other, entry, entry_other, keys):
    heads = query.shape[1]
    return pl.pallas_call(
        attend_kernel,
        out_shape=jax.ShapeDtypeStruct((heads, LATENT_WIDTH), jnp.bfloat16),
        in_specs=[SMEM, VMEM, VMEM, VMEM, VMEM, VMEM],
        out_specs=VMEM,
        compiler_params=pltpu.CompilerParams(vmem_limit_bytes=12 * MIB),
        cost_estimate=FREE,
        name="attend",
    )(in_smem(facts), in_vmem(query), query_other, in_vmem(entry), entry_other, in_vmem(keys))


def project_kernel(
    rank, flags_hbm, per_head, expand_hbm, residual_hbm, weight,
    keep, send, flags, expand, residual, weight_here, values_here, sems, small_sems,
):
    heads, _, width = expand.shape
    rows = per_head.shape[0] // heads
    half = rows // 2
    small = [
        pltpu.make_async_copy(source, target, small_sems.at[index])
        for index, (source, target) in enumerate(
            [(flags_hbm, flags), (expand_hbm, expand), (residual_hbm, residual)]
        )
    ]
    parts = parts_of(weight.shape[1])
    copies = [
        pltpu.make_async_copy(weight.at[:, part], weight_here.at[:, part], sems.at[index])
        for index, part in enumerate(parts)
    ]
    for copy in small + copies:
        copy.start()
    for copy in small:
        copy.wait()
    bit = rank[0] % 2
    place = lax.broadcasted_iota(jnp.int32, (rows, 1), 0)
    source = jnp.zeros((rows, 1), jnp.int32)
    for position in range(rows):
        slot = 2 * position + bit if position < half else 2 * (position - half) + 1 - bit
        row = jnp.where(flags[0, slot] == 1, (slot + half) % rows, slot)
        source = jnp.where(place == position, row, source)
    lanes = lax.broadcasted_iota(jnp.int32, (rows, rows * heads), 1)
    pick = jnp.concatenate(
        [(lanes == source * heads + head).astype(jnp.float32) for head in range(heads)], axis=0
    ).astype(jnp.bfloat16)
    latent = jnp.dot(pick, per_head[...], preferred_element_type=jnp.float32).astype(jnp.bfloat16)
    for head in range(heads):
        values_here[:, head * width : (head + 1) * width] = jnp.dot(
            latent[head * rows : (head + 1) * rows],
            expand[head],
            preferred_element_type=jnp.float32,
        ).astype(jnp.bfloat16)
    mine = lax.broadcasted_iota(jnp.int32, (half, 1), 0) == rank[0] // 2

    for copy, part in zip(copies, parts):
        copy.wait()
        partial = jnp.dot(
            values_here[...], weight_here[:, part], preferred_element_type=jnp.float32
        )
        own = residual[:, part].astype(jnp.float32)
        keep[:, part] = partial[:half] + jnp.where(mine, own, 0.0)
        send[:, part] = partial[half:].astype(jnp.bfloat16)


def each_part(size, count, body):
    part = size // count

    @pl.loop(0, count)
    def _(index):
        body(index, pl.ds(pl.multiple_of(index * part, part), part))


def parts_of(size):
    cuts = [0, size * 4 // 7, size]
    return [pl.ds(low, high - low) for low, high in zip(cuts, cuts[1:])]


def project(rank, flags, per_head, expand, weight, residual):
    rows, (depth, width) = per_head.shape[0] // expand.shape[0], weight.shape
    half = rows // 2
    return pl.pallas_call(
        project_kernel,
        out_shape=(
            jax.ShapeDtypeStruct((half, width), jnp.float32),
            jax.ShapeDtypeStruct((half, width), jnp.bfloat16),
        ),
        in_specs=[SMEM, HBM, VMEM, HBM, HBM, HBM],
        out_specs=(VMEM, VMEM),
        scratch_shapes=[
            pltpu.SMEM(flags.shape, flags.dtype),
            pltpu.VMEM(expand.shape, expand.dtype),
            pltpu.VMEM(residual.shape, residual.dtype),
            pltpu.VMEM(weight.shape, weight.dtype),
            pltpu.VMEM((rows, depth), jnp.bfloat16),
            pltpu.SemaphoreType.DMA((len(parts_of(width)),)),
            pltpu.SemaphoreType.DMA((3,)),
        ],
        compiler_params=pltpu.CompilerParams(vmem_limit_bytes=bytes_of(weight) + 10 * MIB),
        cost_estimate=FREE,
        name="project",
    )(
        rank, in_hbm(flags), per_head, in_hbm(expand), in_hbm(residual), in_hbm(weight)
    )


def add_kernel(keep, arrived, total, send):
    def body(index, here):
        result = keep[:, here] + arrived[:, here].astype(jnp.float32)
        total[:, here] = result
        send[:, here] = result.astype(send.dtype)

    each_part(keep.shape[1], 7, body)


def add(keep, arrived):
    return pl.pallas_call(
        add_kernel,
        out_shape=(
            jax.ShapeDtypeStruct(keep.shape, jnp.float32),
            jax.ShapeDtypeStruct(keep.shape, jnp.bfloat16),
        ),
        in_specs=[VMEM, VMEM],
        out_specs=(VMEM, VMEM),
        compiler_params=pltpu.CompilerParams(vmem_limit_bytes=8 * MIB),
        cost_estimate=FREE,
        name="add",
    )(keep, arrived)


def halve_kernel(keep, arrived, kept, send):
    half = keep.shape[0] // 2

    def body(index, here):
        total = keep[:, here] + arrived[:, here].astype(jnp.float32)
        kept[:, here] = total[:half]
        send[:, here] = total[half:].astype(send.dtype)

    each_part(keep.shape[1], 7, body)


def halve(keep, arrived, cost=FREE):
    shape = (keep.shape[0] // 2, keep.shape[1])
    return pl.pallas_call(
        halve_kernel,
        out_shape=(
            jax.ShapeDtypeStruct(shape, jnp.float32),
            jax.ShapeDtypeStruct(shape, jnp.bfloat16),
        ),
        in_specs=[VMEM, VMEM],
        out_specs=(VMEM, VMEM),
        compiler_params=pltpu.CompilerParams(vmem_limit_bytes=8 * MIB),
        cost_estimate=cost,
        name="halve",
    )(keep, arrived)


def finish_kernel(keep, arrived, out):
    out[...] = (keep[...] + arrived[...].astype(jnp.float32)).astype(out.dtype)


def finish(keep, arrived):
    return pl.pallas_call(
        finish_kernel,
        out_shape=jax.ShapeDtypeStruct(keep.shape, jnp.bfloat16),
        in_specs=[VMEM, VMEM],
        out_specs=VMEM,
        compiler_params=pltpu.CompilerParams(vmem_limit_bytes=8 * MIB),
        cost_estimate=FREE,
        name="finish",
    )(keep, arrived)


def load_kernel(first, source, after, target, sem):
    copy = pltpu.make_async_copy(source.at[pl.ds(first, target.shape[0])], target, sem)
    copy.start()
    copy.wait()


def load(array, first, rows, after):
    return pl.pallas_call(
        functools.partial(load_kernel, first),
        out_shape=pltpu.VMEM((rows, array.shape[1]), array.dtype),
        in_specs=[HBM, ANY],
        out_specs=VMEM,
        scratch_shapes=[pltpu.SemaphoreType.DMA],
        compiler_params=pltpu.CompilerParams(vmem_limit_bytes=MIB),
        cost_estimate=FREE,
        name="load_weight",
    )(in_hbm(array), after)


def norm_kernel(rank, keep, arrived, gain, normed, own, square):
    rows, width = keep.shape
    mine = lax.broadcasted_iota(jnp.int32, (rows, 1), 0) == rank[0] // 2
    square[...] = jnp.zeros_like(square)

    def measure(index, here):
        state = keep[:, here] + arrived[:, here].astype(jnp.float32)
        square[...] += jnp.sum(state * state, axis=1, keepdims=True)
        own[:, here] = jnp.sum(jnp.where(mine, state, 0.0), axis=0, keepdims=True)

    each_part(width, 7, measure)
    scale = lax.rsqrt(square[...] / width + 1e-06)

    def rescale(index, here):
        state = keep[:, here] + arrived[:, here].astype(jnp.float32)
        normed[:, here] = (state * scale * gain[:, here].astype(jnp.float32)).astype(normed.dtype)

    each_part(width, 7, rescale)


def norm(rank, keep, arrived, gain):
    return pl.pallas_call(
        norm_kernel,
        out_shape=(
            jax.ShapeDtypeStruct(keep.shape, jnp.bfloat16),
            jax.ShapeDtypeStruct((1, keep.shape[1]), jnp.float32),
        ),
        in_specs=[SMEM, VMEM, VMEM, VMEM],
        out_specs=(VMEM, VMEM),
        scratch_shapes=[pltpu.VMEM((keep.shape[0], 1), jnp.float32)],
        compiler_params=pltpu.CompilerParams(vmem_limit_bytes=8 * MIB),
        cost_estimate=FREE,
        name="norm",
    )(rank, keep, arrived, gain.reshape(1, -1))


DEPTH = 512
PARTS = 4


def feed_kernel(
    order, rank, mine, other, own, gate, up_low, up_high, down, keep, send, rows_here, down_here,
    hidden_here, sems,
):
    half = mine.shape[0]
    rows = 2 * half
    steps, low = gate.shape[0] // DEPTH, up_low.shape[0] // DEPTH
    width = down.shape[1]
    part = width // PARTS

    def depth(index):
        return pl.ds(pl.multiple_of(index * DEPTH, DEPTH), DEPTH)

    def down_copy(index, here):
        return pltpu.make_async_copy(down.at[:, here], down_here.at[:, here], sems.at[index])

    for index in range(PARTS):
        down_copy(index, pl.ds(index * part, part)).start()

    def place_rows(index, here):
        rows_here[:, here] = jnp.concatenate(
            [mine[:, here].astype(jnp.float32), other[:, here].astype(jnp.float32)], axis=0
        ).astype(jnp.bfloat16)

    each_part(mine.shape[1], 7, place_rows)

    def step(index, total, up_part):
        block = rows_here[:, depth(index)]
        return (
            total[0] + jnp.dot(block, gate[depth(index)], preferred_element_type=jnp.float32),
            total[1] + jnp.dot(block, up_part, preferred_element_type=jnp.float32),
        )

    def low_step(index, total):
        return step(index, total, up_low[depth(index)])

    def high_step(index, total):
        return step(index, total, up_high[depth(index - low)])

    zeros = jnp.zeros((rows, gate.shape[1]), jnp.float32)
    total = lax.fori_loop(0, low, low_step, (zeros, zeros))
    gated, upper = lax.fori_loop(low, steps, high_step, total)
    hidden = (gated * jax.nn.sigmoid(gated) * upper).astype(jnp.bfloat16)

    place = lax.broadcasted_iota(jnp.int32, (rows, 1), 0)
    source = jnp.zeros((rows, 1), jnp.int32)
    for position in range(rows):
        inner = position % half
        other_bits = sum(
            (inner >> len(order) - 1 - index & 1) << bit - 1 for index, bit in enumerate(order)
        )
        row = position - inner + ((rank[0] // 2) ^ other_bits)
        source = jnp.where(place == position, row, source)
    pick = (lax.broadcasted_iota(jnp.int32, (rows, rows), 1) == source).astype(jnp.bfloat16)
    hidden_here[...] = jnp.dot(pick, hidden, preferred_element_type=jnp.float32).astype(
        jnp.bfloat16
    )

    first = lax.broadcasted_iota(jnp.int32, (half, 1), 0) == 0

    def project_down(index, here):
        down_copy(index, here).wait()
        total = jnp.dot(hidden_here[...], down_here[:, here], preferred_element_type=jnp.float32)
        keep[:, here] = total[:half] + jnp.where(first, own[:, here], 0.0)
        send[:, here] = total[half:].astype(jnp.bfloat16)

    each_part(width, PARTS, project_down)


def feed(order, rank, mine, other, own, gate, up_low, up_high, down):
    half, width = mine.shape[0], down.shape[1]
    return pl.pallas_call(
        functools.partial(feed_kernel, order),
        out_shape=(
            jax.ShapeDtypeStruct((half, width), jnp.float32),
            jax.ShapeDtypeStruct((half, width), jnp.bfloat16),
        ),
        in_specs=[SMEM, VMEM, VMEM, VMEM, VMEM, VMEM, VMEM, HBM],
        out_specs=(VMEM, VMEM),
        scratch_shapes=[
            pltpu.VMEM((2 * half, mine.shape[1]), jnp.bfloat16),
            pltpu.VMEM(down.shape, down.dtype),
            pltpu.VMEM((2 * half, down.shape[0]), jnp.bfloat16),
            pltpu.SemaphoreType.DMA((PARTS,)),
        ],
        compiler_params=pltpu.CompilerParams(vmem_limit_bytes=bytes_of(down) + 6 * MIB),
        cost_estimate=FREE,
        name="feed",
    )(rank, mine, other, own, in_vmem(gate), in_vmem(up_low), in_vmem(up_high), in_hbm(down))


def hold_kernel(
    rank, lengths, flags, entry, own, early, late, held, block, fetched, stored
):
    slot = rank[0]
    ranks = lengths.shape[0]
    swapped = flags[0, slot] == 1
    position = lengths[jnp.where(swapped, (slot + ranks // 2) % ranks, slot)]

    cut = early.shape[0]
    size = late.shape[0] // 3
    parts = [pl.ds(0, cut), *(pl.ds(cut + size * index, size) for index in range(3))]

    @pl.when(swapped)
    def _():
        pltpu.make_async_copy(early, block.at[parts[0]], fetched.at[0]).start()
        for index, part in enumerate(parts[1:]):
            source = late.at[pl.ds(size * index, size)]
            pltpu.make_async_copy(source, block.at[part], fetched.at[index + 1]).start()

    @pl.when(jnp.logical_not(swapped))
    def _():
        for index, part in enumerate(parts):
            pltpu.make_async_copy(own.at[part], block.at[part], fetched.at[index]).start()

    column = entry[...].astype(jnp.float32).T.astype(block.dtype)
    tile = position // 128
    here = pl.ds(pl.multiple_of(tile * 128, 128), 128)
    stores = []
    for index, part in enumerate(parts):
        pltpu.make_async_copy(own.at[part], block.at[part], fetched.at[index]).wait()
        column_part = column[part.start : part.start + part.size]
        lanes = lax.broadcasted_iota(jnp.int32, (part.size, 128), 1)
        block[part, here] = jnp.where(lanes == position - tile * 128, column_part, block[part, here])
        store = pltpu.make_async_copy(block.at[part], held.at[part], stored.at[index])
        store.start()
        stores.append(store)
    for store in stores:
        store.wait()


def hold(rank, lengths, flags, entry, own, early, late):
    return pl.pallas_call(
        hold_kernel,
        out_shape=jax.ShapeDtypeStruct(own.shape, own.dtype),
        in_specs=[SMEM, SMEM, SMEM, VMEM, HBM, HBM, HBM],
        out_specs=ANY,
        scratch_shapes=[
            pltpu.VMEM(own.shape, own.dtype),
            pltpu.SemaphoreType.DMA((5,)),
            pltpu.SemaphoreType.DMA((5,)),
        ],
        compiler_params=pltpu.CompilerParams(vmem_limit_bytes=6 * MIB),
        cost_estimate=FREE,
        name="hold",
    )(rank, lengths, flags, entry, in_hbm(own), in_hbm(early), in_hbm(late))


def local(
    cache,
    lengths,
    swap_flags,
    queries,
    latents,
    residual,
    norm_gain,
    value_expand_weight,
    out_proj,
    gate_weight,
    up_weight,
    down_weight,
):
    ranks = lax.axis_size(AXES)
    bits = ranks.bit_length() - 1
    top = bits - 1
    rank = lax.axis_index(AXES)
    here = rank.reshape(1)
    keys = jnp.swapaxes(cache[0], 0, 1)
    query = jnp.swapaxes(queries[0, 0], 0, 1)
    entry = latents[0]

    query_other = swap_bit(query, top)
    entry_other = swap_bit(entry, top)
    facts, swapped, movers, *kept, early, late = prepare(
        here, lengths, swap_flags, query, entry, keys
    )
    query_other, facts, swapped, movers, *kept = lax.optimization_barrier(
        (query_other, facts, swapped, movers, *kept)
    )
    query_here, entry_here, keys_here = kept
    context = attend(facts, query_here, query_other, entry_here, entry_other, keys_here)

    heads = context.shape[0] // ranks
    per_head = lax.all_to_all(
        context.reshape(ranks, heads, LATENT_WIDTH), AXES, split_axis=0, concat_axis=0, tiled=True
    ).reshape(ranks * heads, LATENT_WIDTH)
    per_head, swapped = lax.optimization_barrier((per_head, swapped))
    def projected(per_head):
        return project(here, swap_flags, per_head, value_expand_weight, out_proj, residual[0])

    def moving(per_head):
        early_other = swap_bit(early, top)
        return *projected(per_head), early_other

    def staying(per_head):
        return *projected(per_head), jnp.zeros_like(early)

    keep, send, early_other = lax.cond(swapped[0] == 1, moving, staying, per_head)

    keep, send = add(keep, swap_bit(send, 0))
    send, movers = lax.optimization_barrier((send, movers))
    depth = up_weight.shape[0]
    low = depth * 4 // 7 // DEPTH * DEPTH
    for bit in reversed(range(2, bits)):
        arrived = swap_bit(send, bit)
        if bit == top:
            up_low = load(up_weight, 0, low, send)
            arrived, up_low = lax.optimization_barrier((arrived, up_low))
        keep, send = add(keep, arrived)

    order = [1, top, *range(2, top)]

    def near(keep, send, up_low):
        arrived = swap_bit(send, 1)
        up_high = load(up_weight, low, depth - low, send)
        arrived, up_high = lax.optimization_barrier((arrived, up_high))
        normed, own = norm(here, keep, arrived, norm_gain)
        keep, send = feed(
            order, here, normed, swap_bit(normed, 0), own, gate_weight, up_low, up_high, down_weight
        )
        keep, send = halve(keep, swap_bit(send, 0))
        keep, send = halve(keep, swap_bit(send, 1))
        return keep, swap_bit(send, top)

    def beside(movers):
        def branch(keep, send, up_low):
            if not movers:
                return *halve(*near(keep, send, up_low)), jnp.zeros_like(late)
            late_other = swap_bit(late, top, lambda rank: movers >> rank % 4 & 1)
            some = keep[: keep.shape[0] // 4]
            keep, arrived = lax.cond(
                lengths[0] > 0,
                near,
                lambda *_: (some, some.astype(jnp.bfloat16)),
                keep,
                send,
                up_low,
            )
            keep, send = halve(keep, arrived, LONG)
            late_other, _ = lax.optimization_barrier((late_other, send))
            return keep, send, late_other

        return branch

    keep, send, late_other = lax.switch(
        movers[0], [beside(movers) for movers in range(16)], keep, send, up_low
    )

    for bit in range(2, top - 1):
        keep, send = halve(keep, swap_bit(send, bit))
    layer_out = finish(keep, swap_bit(send, top - 1))
    held = hold(here, lengths, swap_flags, entry, keys, early_other, late_other)
    return layer_out[None], jnp.swapaxes(held, 0, 1)[None]


def solution(mesh):
    placed = (
        P(("groups", "dp", "tp"), None, None),
        P("groups"),
        P(None, "groups"),
        P(None, ("groups", "dp", "tp"), None, None),
        P(None, ("groups", "dp", "tp"), None),
        P(None, ("groups", "dp", "tp"), None),
        P(),
        P(("dp", "tp"), None, None),
        P(("dp", "tp"), None),
        P(None, ("dp", "tp")),
        P(None, ("dp", "tp")),
        P(("dp", "tp"), None),
    )
    return jax.shard_map(
        local,
        mesh=mesh,
        in_specs=placed,
        out_specs=(P(None, ("groups", "dp", "tp"), None), P(("groups", "dp", "tp"), None, None)),
        check_vma=False,
    )
```

```python
import functools

import jax
import jax.numpy as jnp
from jax import lax
from jax.experimental import pallas as pl
from jax.experimental.pallas import tpu as pltpu
from jax.sharding import PartitionSpec as P

LATENT_WIDTH = 512
AXES = ("dp", "tp")
MIB = 1 << 20

VMEM = pl.BlockSpec(memory_space=pltpu.VMEM)
SMEM = pl.BlockSpec(memory_space=pltpu.SMEM)
ANY = pl.BlockSpec(memory_space=pl.ANY)
HBM = pl.BlockSpec(memory_space=pltpu.HBM)

FREE = pl.CostEstimate(flops=0, bytes_accessed=0, transcendentals=0)

LONG = pl.CostEstimate(flops=10**12, bytes_accessed=10**9, transcendentals=0)

score_scale = 0.07216878364870322


def in_vmem(array):
    return pltpu.with_memory_space_constraint(array, pltpu.VMEM)


def in_smem(array):
    return pltpu.with_memory_space_constraint(array, pltpu.SMEM)


def in_hbm(array):
    return pltpu.with_memory_space_constraint(array, pltpu.HBM)


def bytes_of(*arrays):
    return sum(array.size * array.dtype.itemsize for array in arrays)


def swap_bit(block, bit, take=lambda rank: True):
    ranks = lax.axis_size(AXES)
    route = [(rank, rank ^ 1 << bit) for rank in range(ranks) if take(rank)]
    return lax.ppermute(block, AXES, route)


def prepare_kernel(
    rank, lengths_hbm, flags_hbm, query_hbm, entry_hbm, keys_hbm,
    facts, swapped, movers, query, entry, keys, early, late, lengths, flags, sems,
):
    copies = [
        pltpu.make_async_copy(source, target, sems.at[index])
        for index, (source, target) in enumerate(
            [
                (lengths_hbm, lengths),
                (flags_hbm, flags),
                (query_hbm, query),
                (entry_hbm, entry),
                (keys_hbm, keys),
            ]
        )
    ]
    for copy in copies:
        copy.start()
    for copy in copies[:2]:
        copy.wait()
    slot = rank[0]
    facts[0] = lengths[slot]
    facts[1] = flags[0, slot]
    swapped[0] = flags[0, slot]
    first = slot // 4 * 4
    movers[0] = sum(flags[0, first + each] * (1 << each) for each in range(4))
    for copy in copies[2:]:
        copy.wait()
    rows = early.shape[0]
    parts = [
        pltpu.make_async_copy(keys.at[pl.ds(0, rows)], early, sems.at[0]),
        pltpu.make_async_copy(keys.at[pl.ds(rows, late.shape[0])], late, sems.at[1]),
    ]
    for copy in parts:
        copy.start()
    for copy in parts:
        copy.wait()


EARLY = 96


def prepare(rank, lengths, flags, query, entry, keys):
    return pl.pallas_call(
        prepare_kernel,
        out_shape=(
            pltpu.SMEM((2,), jnp.int32),
            jax.ShapeDtypeStruct((1,), jnp.int32),
            jax.ShapeDtypeStruct((1,), jnp.int32),
            pltpu.VMEM(query.shape, query.dtype),
            pltpu.VMEM(entry.shape, entry.dtype),
            pltpu.VMEM(keys.shape, keys.dtype),
            pltpu.HBM((EARLY, keys.shape[1]), keys.dtype),
            pltpu.HBM((keys.shape[0] - EARLY, keys.shape[1]), keys.dtype),
        ),
        in_specs=[SMEM, HBM, HBM, HBM, HBM, HBM],
        out_specs=(SMEM, SMEM, SMEM, VMEM, VMEM, VMEM, HBM, HBM),
        scratch_shapes=[
            pltpu.SMEM(lengths.shape, lengths.dtype),
            pltpu.SMEM(flags.shape, flags.dtype),
            pltpu.SemaphoreType.DMA((5,)),
        ],
        compiler_params=pltpu.CompilerParams(vmem_limit_bytes=MIB),
        cost_estimate=FREE,
        name="prepare",
    )(rank, in_hbm(lengths), in_hbm(flags), in_hbm(query), in_hbm(entry), in_hbm(keys))


def attend_kernel(facts, query, query_other, entry, entry_other, keys, context):
    live = facts[0]
    swapped = facts[1] == 1
    new_wide = jnp.where(
        swapped, entry_other[...].astype(jnp.float32), entry[...].astype(jnp.float32)
    )
    rows = jnp.where(swapped, query_other[...], query[...]).T
    new_score = jnp.sum(rows.astype(jnp.float32) * new_wide, axis=1, keepdims=True)
    keys_now = keys[...]
    scores = jnp.dot(rows, keys_now, preferred_element_type=jnp.float32)
    positions = lax.broadcasted_iota(jnp.int32, scores.shape, 1)
    scores = jnp.where(positions == live, new_score, scores) * score_scale
    scores = jnp.where(positions <= live, scores, -1e30)
    top = jnp.max(scores, axis=1, keepdims=True)
    weights = jnp.where(positions <= live, jnp.exp(scores - top), 0.0)
    total = jnp.sum(weights, axis=1, keepdims=True)
    probs = (weights / total).astype(jnp.bfloat16)
    new_prob = (jnp.exp(new_score * score_scale - top) / total).astype(jnp.bfloat16)
    probs = jnp.where(positions == live, jnp.zeros_like(probs), probs)
    result = lax.dot_general(
        probs,
        keys_now[:LATENT_WIDTH],
        (((1,), (1,)), ((), ())),
        preferred_element_type=jnp.float32,
    )
    result = result + new_prob.astype(jnp.float32) * new_wide[:, :LATENT_WIDTH]
    context[...] = result.astype(jnp.bfloat16)


def attend(facts, query, query_other, entry, entry_other, keys):
    heads = query.shape[1]
    return pl.pallas_call(
        attend_kernel,
        out_shape=jax.ShapeDtypeStruct((heads, LATENT_WIDTH), jnp.bfloat16),
        in_specs=[SMEM, VMEM, VMEM, VMEM, VMEM, VMEM],
        out_specs=VMEM,
        compiler_params=pltpu.CompilerParams(vmem_limit_bytes=12 * MIB),
        cost_estimate=FREE,
        name="attend",
    )(in_smem(facts), in_vmem(query), query_other, in_vmem(entry), entry_other, in_vmem(keys))


def project_kernel(
    rank, flags_hbm, per_head, expand_hbm, residual_hbm, weight,
    keep, send, flags, expand, residual, weight_here, values_here, sems, small_sems,
):
    heads, _, width = expand.shape
    rows = per_head.shape[0] // heads
    half = rows // 2
    small = [
        pltpu.make_async_copy(source, target, small_sems.at[index])
        for index, (source, target) in enumerate(
            [(flags_hbm, flags), (expand_hbm, expand), (residual_hbm, residual)]
        )
    ]
    parts = parts_of(weight.shape[1])
    copies = [
        pltpu.make_async_copy(weight.at[:, part], weight_here.at[:, part], sems.at[index])
        for index, part in enumerate(parts)
    ]
    for copy in small + copies:
        copy.start()
    for copy in small:
        copy.wait()
    bit = rank[0] % 2
    place = lax.broadcasted_iota(jnp.int32, (rows, 1), 0)
    source = jnp.zeros((rows, 1), jnp.int32)
    for position in range(rows):
        slot = 2 * position + bit if position < half else 2 * (position - half) + 1 - bit
        row = jnp.where(flags[0, slot] == 1, (slot + half) % rows, slot)
        source = jnp.where(place == position, row, source)
    lanes = lax.broadcasted_iota(jnp.int32, (rows, rows * heads), 1)
    pick = jnp.concatenate(
        [(lanes == source * heads + head).astype(jnp.float32) for head in range(heads)], axis=0
    ).astype(jnp.bfloat16)
    latent = jnp.dot(pick, per_head[...], preferred_element_type=jnp.float32).astype(jnp.bfloat16)
    for head in range(heads):
        values_here[:, head * width : (head + 1) * width] = jnp.dot(
            latent[head * rows : (head + 1) * rows],
            expand[head],
            preferred_element_type=jnp.float32,
        ).astype(jnp.bfloat16)
    mine = lax.broadcasted_iota(jnp.int32, (half, 1), 0) == rank[0] // 2

    for copy, part in zip(copies, parts):
        copy.wait()
        partial = jnp.dot(
            values_here[...], weight_here[:, part], preferred_element_type=jnp.float32
        )
        own = residual[:, part].astype(jnp.float32)
        keep[:, part] = partial[:half] + jnp.where(mine, own, 0.0)
        send[:, part] = partial[half:].astype(jnp.bfloat16)


def each_part(size, count, body):
    part = size // count

    @pl.loop(0, count)
    def _(index):
        body(index, pl.ds(pl.multiple_of(index * part, part), part))


def parts_of(size):
    cuts = [0, size * 4 // 7, size]
    return [pl.ds(low, high - low) for low, high in zip(cuts, cuts[1:])]


def project(rank, flags, per_head, expand, weight, residual):
    rows, (depth, width) = per_head.shape[0] // expand.shape[0], weight.shape
    half = rows // 2
    return pl.pallas_call(
        project_kernel,
        out_shape=(
            jax.ShapeDtypeStruct((half, width), jnp.float32),
            jax.ShapeDtypeStruct((half, width), jnp.bfloat16),
        ),
        in_specs=[SMEM, HBM, VMEM, HBM, HBM, HBM],
        out_specs=(VMEM, VMEM),
        scratch_shapes=[
            pltpu.SMEM(flags.shape, flags.dtype),
            pltpu.VMEM(expand.shape, expand.dtype),
            pltpu.VMEM(residual.shape, residual.dtype),
            pltpu.VMEM(weight.shape, weight.dtype),
            pltpu.VMEM((rows, depth), jnp.bfloat16),
            pltpu.SemaphoreType.DMA((len(parts_of(width)),)),
            pltpu.SemaphoreType.DMA((3,)),
        ],
        compiler_params=pltpu.CompilerParams(vmem_limit_bytes=bytes_of(weight) + 10 * MIB),
        cost_estimate=FREE,
        name="project",
    )(
        rank, in_hbm(flags), per_head, in_hbm(expand), in_hbm(residual), in_hbm(weight)
    )


def add_kernel(keep, arrived, total, send):
    def body(index, here):
        result = keep[:, here] + arrived[:, here].astype(jnp.float32)
        total[:, here] = result
        send[:, here] = result.astype(send.dtype)

    each_part(keep.shape[1], 7, body)


def add(keep, arrived):
    return pl.pallas_call(
        add_kernel,
        out_shape=(
            jax.ShapeDtypeStruct(keep.shape, jnp.float32),
            jax.ShapeDtypeStruct(keep.shape, jnp.bfloat16),
        ),
        in_specs=[VMEM, VMEM],
        out_specs=(VMEM, VMEM),
        compiler_params=pltpu.CompilerParams(vmem_limit_bytes=8 * MIB),
        cost_estimate=FREE,
        name="add",
    )(keep, arrived)


def halve_kernel(keep, arrived, kept, send):
    half = keep.shape[0] // 2

    def body(index, here):
        total = keep[:, here] + arrived[:, here].astype(jnp.float32)
        kept[:, here] = total[:half]
        send[:, here] = total[half:].astype(send.dtype)

    each_part(keep.shape[1], 7, body)


def halve(keep, arrived, cost=FREE):
    shape = (keep.shape[0] // 2, keep.shape[1])
    return pl.pallas_call(
        halve_kernel,
        out_shape=(
            jax.ShapeDtypeStruct(shape, jnp.float32),
            jax.ShapeDtypeStruct(shape, jnp.bfloat16),
        ),
        in_specs=[VMEM, VMEM],
        out_specs=(VMEM, VMEM),
        compiler_params=pltpu.CompilerParams(vmem_limit_bytes=8 * MIB),
        cost_estimate=cost,
        name="halve",
    )(keep, arrived)


def split_kernel(total, kept, send):
    half = total.shape[0] // 2
    kept[...] = total[:half]
    send[...] = total[half:].astype(send.dtype)


def split(total, cost=FREE):
    shape = (total.shape[0] // 2, total.shape[1])
    return pl.pallas_call(
        split_kernel,
        out_shape=(
            jax.ShapeDtypeStruct(shape, jnp.float32),
            jax.ShapeDtypeStruct(shape, jnp.bfloat16),
        ),
        in_specs=[VMEM],
        out_specs=(VMEM, VMEM),
        compiler_params=pltpu.CompilerParams(vmem_limit_bytes=4 * MIB),
        cost_estimate=cost,
        name="split",
    )(total)


def finish_kernel(keep, arrived, out):
    out[...] = (keep[...] + arrived[...].astype(jnp.float32)).astype(out.dtype)


def finish(keep, arrived):
    return pl.pallas_call(
        finish_kernel,
        out_shape=jax.ShapeDtypeStruct(keep.shape, jnp.bfloat16),
        in_specs=[VMEM, VMEM],
        out_specs=VMEM,
        compiler_params=pltpu.CompilerParams(vmem_limit_bytes=8 * MIB),
        cost_estimate=FREE,
        name="finish",
    )(keep, arrived)


def load_kernel(first, source, after, target, sem):
    copy = pltpu.make_async_copy(source.at[pl.ds(first, target.shape[0])], target, sem)
    copy.start()
    copy.wait()


def load(array, first, rows, after):
    return pl.pallas_call(
        functools.partial(load_kernel, first),
        out_shape=pltpu.VMEM((rows, array.shape[1]), array.dtype),
        in_specs=[HBM, ANY],
        out_specs=VMEM,
        scratch_shapes=[pltpu.SemaphoreType.DMA],
        compiler_params=pltpu.CompilerParams(vmem_limit_bytes=MIB),
        cost_estimate=FREE,
        name="load_weight",
    )(in_hbm(array), after)


def norm_kernel(rank, keep, arrived, gain, normed, own, square):
    rows, width = keep.shape
    mine = lax.broadcasted_iota(jnp.int32, (rows, 1), 0) == rank[0] // 2
    square[...] = jnp.zeros_like(square)

    def measure(index, here):
        state = keep[:, here] + arrived[:, here].astype(jnp.float32)
        square[...] += jnp.sum(state * state, axis=1, keepdims=True)
        own[:, here] = jnp.sum(jnp.where(mine, state, 0.0), axis=0, keepdims=True)

    each_part(width, 7, measure)
    scale = lax.rsqrt(square[...] / width + 1e-06)

    def rescale(index, here):
        state = keep[:, here] + arrived[:, here].astype(jnp.float32)
        normed[:, here] = (state * scale * gain[:, here].astype(jnp.float32)).astype(normed.dtype)

    each_part(width, 7, rescale)


def norm(rank, keep, arrived, gain):
    return pl.pallas_call(
        norm_kernel,
        out_shape=(
            jax.ShapeDtypeStruct(keep.shape, jnp.bfloat16),
            jax.ShapeDtypeStruct((1, keep.shape[1]), jnp.float32),
        ),
        in_specs=[SMEM, VMEM, VMEM, VMEM],
        out_specs=(VMEM, VMEM),
        scratch_shapes=[pltpu.VMEM((keep.shape[0], 1), jnp.float32)],
        compiler_params=pltpu.CompilerParams(vmem_limit_bytes=8 * MIB),
        cost_estimate=FREE,
        name="norm",
    )(rank, keep, arrived, gain.reshape(1, -1))


DEPTH = 512
PARTS = 4


def feed_kernel(
    order, rank, mine, other, own, gate, up_low, up_high, down, keep, send, rows_here, down_here,
    hidden_here, sems,
):
    half = mine.shape[0]
    rows = 2 * half
    steps, low = gate.shape[0] // DEPTH, up_low.shape[0] // DEPTH
    width = down.shape[1]
    part = width // PARTS

    def depth(index):
        return pl.ds(pl.multiple_of(index * DEPTH, DEPTH), DEPTH)

    def down_copy(index, here):
        return pltpu.make_async_copy(down.at[:, here], down_here.at[:, here], sems.at[index])

    for index in range(PARTS):
        down_copy(index, pl.ds(index * part, part)).start()

    def place_rows(index, here):
        rows_here[:, here] = jnp.concatenate(
            [mine[:, here].astype(jnp.float32), other[:, here].astype(jnp.float32)], axis=0
        ).astype(jnp.bfloat16)

    each_part(mine.shape[1], 7, place_rows)

    def step(index, total, up_part):
        block = rows_here[:, depth(index)]
        return (
            total[0] + jnp.dot(block, gate[depth(index)], preferred_element_type=jnp.float32),
            total[1] + jnp.dot(block, up_part, preferred_element_type=jnp.float32),
        )

    def low_step(index, total):
        return step(index, total, up_low[depth(index)])

    def high_step(index, total):
        return step(index, total, up_high[depth(index - low)])

    zeros = jnp.zeros((rows, gate.shape[1]), jnp.float32)
    total = lax.fori_loop(0, low, low_step, (zeros, zeros))
    gated, upper = lax.fori_loop(low, steps, high_step, total)
    hidden = (gated * jax.nn.sigmoid(gated) * upper).astype(jnp.bfloat16)

    place = lax.broadcasted_iota(jnp.int32, (rows, 1), 0)
    source = jnp.zeros((rows, 1), jnp.int32)
    for position in range(rows):
        inner = position % half
        other_bits = sum(
            (inner >> len(order) - 1 - index & 1) << bit - 1 for index, bit in enumerate(order)
        )
        row = position - inner + ((rank[0] // 2) ^ other_bits)
        source = jnp.where(place == position, row, source)
    pick = (lax.broadcasted_iota(jnp.int32, (rows, rows), 1) == source).astype(jnp.bfloat16)
    hidden_here[...] = jnp.dot(pick, hidden, preferred_element_type=jnp.float32).astype(
        jnp.bfloat16
    )

    first = lax.broadcasted_iota(jnp.int32, (half, 1), 0) == 0

    def project_down(index, here):
        down_copy(index, here).wait()
        total = jnp.dot(hidden_here[...], down_here[:, here], preferred_element_type=jnp.float32)
        keep[:, here] = total[:half] + jnp.where(first, own[:, here], 0.0)
        send[:, here] = total[half:].astype(jnp.bfloat16)

    each_part(width, PARTS, project_down)


def feed(order, rank, mine, other, own, gate, up_low, up_high, down):
    half, width = mine.shape[0], down.shape[1]
    return pl.pallas_call(
        functools.partial(feed_kernel, order),
        out_shape=(
            jax.ShapeDtypeStruct((half, width), jnp.float32),
            jax.ShapeDtypeStruct((half, width), jnp.bfloat16),
        ),
        in_specs=[SMEM, VMEM, VMEM, VMEM, VMEM, VMEM, VMEM, HBM],
        out_specs=(VMEM, VMEM),
        scratch_shapes=[
            pltpu.VMEM((2 * half, mine.shape[1]), jnp.bfloat16),
            pltpu.VMEM(down.shape, down.dtype),
            pltpu.VMEM((2 * half, down.shape[0]), jnp.bfloat16),
            pltpu.SemaphoreType.DMA((PARTS,)),
        ],
        compiler_params=pltpu.CompilerParams(vmem_limit_bytes=bytes_of(down) + 6 * MIB),
        cost_estimate=FREE,
        name="feed",
    )(rank, mine, other, own, in_vmem(gate), in_vmem(up_low), in_vmem(up_high), in_hbm(down))


def hold_kernel(
    rank, lengths, flags, entry, own, early, late, held, block, fetched, stored
):
    slot = rank[0]
    ranks = lengths.shape[0]
    swapped = flags[0, slot] == 1
    position = lengths[jnp.where(swapped, (slot + ranks // 2) % ranks, slot)]

    cut = early.shape[0]
    size = late.shape[0] // 3
    parts = [pl.ds(0, cut), *(pl.ds(cut + size * index, size) for index in range(3))]

    @pl.when(swapped)
    def _():
        pltpu.make_async_copy(early, block.at[parts[0]], fetched.at[0]).start()
        for index, part in enumerate(parts[1:]):
            source = late.at[pl.ds(size * index, size)]
            pltpu.make_async_copy(source, block.at[part], fetched.at[index + 1]).start()

    @pl.when(jnp.logical_not(swapped))
    def _():
        for index, part in enumerate(parts):
            pltpu.make_async_copy(own.at[part], block.at[part], fetched.at[index]).start()

    column = entry[...].astype(jnp.float32).T.astype(block.dtype)
    tile = position // 128
    here = pl.ds(pl.multiple_of(tile * 128, 128), 128)
    stores = []
    for index, part in enumerate(parts):
        pltpu.make_async_copy(own.at[part], block.at[part], fetched.at[index]).wait()
        column_part = column[part.start : part.start + part.size]
        lanes = lax.broadcasted_iota(jnp.int32, (part.size, 128), 1)
        block[part, here] = jnp.where(lanes == position - tile * 128, column_part, block[part, here])
        store = pltpu.make_async_copy(block.at[part], held.at[part], stored.at[index])
        store.start()
        stores.append(store)
    for store in stores:
        store.wait()


def hold(rank, lengths, flags, entry, own, early, late):
    return pl.pallas_call(
        hold_kernel,
        out_shape=jax.ShapeDtypeStruct(own.shape, own.dtype),
        in_specs=[SMEM, SMEM, SMEM, VMEM, HBM, HBM, HBM],
        out_specs=ANY,
        scratch_shapes=[
            pltpu.VMEM(own.shape, own.dtype),
            pltpu.SemaphoreType.DMA((5,)),
            pltpu.SemaphoreType.DMA((5,)),
        ],
        compiler_params=pltpu.CompilerParams(vmem_limit_bytes=6 * MIB),
        cost_estimate=FREE,
        name="hold",
    )(rank, lengths, flags, entry, in_hbm(own), in_hbm(early), in_hbm(late))


def local(
    cache,
    lengths,
    swap_flags,
    queries,
    latents,
    residual,
    norm_gain,
    value_expand_weight,
    out_proj,
    gate_weight,
    up_weight,
    down_weight,
):
    ranks = lax.axis_size(AXES)
    bits = ranks.bit_length() - 1
    top = bits - 1
    rank = lax.axis_index(AXES)
    here = rank.reshape(1)
    keys = jnp.swapaxes(cache[0], 0, 1)
    query = jnp.swapaxes(queries[0, 0], 0, 1)
    entry = latents[0]

    query_other = swap_bit(query, top)
    entry_other = swap_bit(entry, top)
    facts, swapped, movers, *kept, early, late = prepare(
        here, lengths, swap_flags, query, entry, keys
    )
    query_other, facts, swapped, movers, *kept = lax.optimization_barrier(
        (query_other, facts, swapped, movers, *kept)
    )
    query_here, entry_here, keys_here = kept
    context = attend(facts, query_here, query_other, entry_here, entry_other, keys_here)

    heads = context.shape[0] // ranks
    per_head = lax.all_to_all(
        context.reshape(ranks, heads, LATENT_WIDTH), AXES, split_axis=0, concat_axis=0, tiled=True
    ).reshape(ranks * heads, LATENT_WIDTH)
    per_head, swapped = lax.optimization_barrier((per_head, swapped))
    def projected(per_head):
        return project(here, swap_flags, per_head, value_expand_weight, out_proj, residual[0])

    def moving(per_head):
        early_other = swap_bit(early, top)
        return *projected(per_head), early_other

    def staying(per_head):
        return *projected(per_head), jnp.zeros_like(early)

    keep, send, early_other = lax.cond(swapped[0] == 1, moving, staying, per_head)

    keep, send = add(keep, swap_bit(send, 0))
    send, movers = lax.optimization_barrier((send, movers))
    depth = up_weight.shape[0]
    low = depth * 4 // 7 // DEPTH * DEPTH
    for bit in reversed(range(2, bits)):
        arrived = swap_bit(send, bit)
        if bit == top:
            up_low = load(up_weight, 0, low, send)
            arrived, up_low = lax.optimization_barrier((arrived, up_low))
        keep, send = add(keep, arrived)

    order = [1, top, *range(2, top)]

    def near(keep, send, up_low):
        arrived = swap_bit(send, 1)
        up_high = load(up_weight, low, depth - low, send)
        arrived, up_high = lax.optimization_barrier((arrived, up_high))
        normed, own = norm(here, keep, arrived, norm_gain)
        keep, send = feed(
            order, here, normed, swap_bit(normed, 0), own, gate_weight, up_low, up_high, down_weight
        )
        keep, send = halve(keep, swap_bit(send, 0))
        keep, send = halve(keep, swap_bit(send, 1))
        return add(keep, swap_bit(send, top))[0]

    def beside(movers):
        def branch(keep, send, up_low):
            if not movers:
                return *split(near(keep, send, up_low)), jnp.zeros_like(late)
            late_other = swap_bit(late, top, lambda rank: movers >> rank % 4 & 1)
            some = keep[: keep.shape[0] // 4]
            total = lax.cond(
                lengths[0] > 0,
                near,
                lambda *_: some,
                keep,
                send,
                up_low,
            )
            keep, send = split(total, LONG)
            late_other, _ = lax.optimization_barrier((late_other, send))
            return keep, send, late_other

        return branch

    keep, send, late_other = lax.switch(
        movers[0], [beside(movers) for movers in range(16)], keep, send, up_low
    )

    for bit in range(2, top - 1):
        keep, send = halve(keep, swap_bit(send, bit))
    layer_out = finish(keep, swap_bit(send, top - 1))
    held = hold(here, lengths, swap_flags, entry, keys, early_other, late_other)
    return layer_out[None], jnp.swapaxes(held, 0, 1)[None]


def solution(mesh):
    placed = (
        P(("groups", "dp", "tp"), None, None),
        P("groups"),
        P(None, "groups"),
        P(None, ("groups", "dp", "tp"), None, None),
        P(None, ("groups", "dp", "tp"), None),
        P(None, ("groups", "dp", "tp"), None),
        P(),
        P(("dp", "tp"), None, None),
        P(("dp", "tp"), None),
        P(None, ("dp", "tp")),
        P(None, ("dp", "tp")),
        P(("dp", "tp"), None),
    )
    return jax.shard_map(
        local,
        mesh=mesh,
        in_specs=placed,
        out_specs=(P(None, ("groups", "dp", "tp"), None), P(("groups", "dp", "tp"), None, None)),
        check_vma=False,
    )
```
